32 devices in a mesh: ctx: 8 (over y, x, core), head: 4 (over z).
Axes of the slice: x: 2, y: 2, z: 4, core: 2. Of those that a mesh axis runs over, the one named last changes fastest.
Arguments:
- features: bfloat16 [4096, 8192], P('ctx', 'head'), may hold values from -6 to 6
- gate_values: bfloat16 [4096, 8192], P('ctx', 'head'), may hold values from -6 to 6
- write_proj: bfloat16 [4096, 1024], P('ctx', 'head'), may hold values from -0.0234375 to 0.0234375
- read_proj: bfloat16 [4096, 1024], P('ctx', 'head'), may hold values from -6 to 6
- step_size: float32 [128, 4096], P('head', 'ctx'), may hold values from 0.25 to 2
- log_decay: float32 [128, 4096], P('head', 'ctx'), may hold values from -1 to 0
- starts: int32 [4096], P('ctx'), may hold values from 0 to 1
- skip_weight: float32 [128], P('head'), may hold values from 0.5 to 1.5
- norm_gain: float32 [8192], P('head'), may hold values from 0.1 to 1.9
- out_weight: bfloat16 [8192, 4096], P('head'), may hold values from -0.0625 to 0.0625
Outputs:
- mixed: bfloat16 [4096, 4096], P(('ctx', 'head'))
The draws below stay inside these ranges and needn't reach their ends.
All inputs are finite; a program needn't handle non-finite values.
Results may differ from the reference program's by a relative error of at most 0.0061.
Values sent between devices are 32-bit elements; how exact they have to be, the bound alone decides.
No kernel may reach another device: no remote copies, remote signals or barrier semaphores. Data moves between devices by JAX's collectives and lax.ppermute only.
A program may use at most 128 MiB of HBM per device.

```python
import math
import jax
import jax.numpy as jnp
from jax import lax

D = 4096
HEADS = 128
HEAD_DIM = 64
NSTATE = 128
GROUPS = 8
SPAN = 256
TOK_DEV = 512
SEQUENCE_SPAN = 4096
INNER = 8192


def draw_log_decay(key, part):
    floor_offset = jax.random.fold_in(key, 7)
    seed_selection, seed_gradual, seed_quick, seed_jagged, seed_spike, seed_extent = jax.random.split(floor_offset, 6)
    slow_rate = jnp.exp(jax.random.uniform(seed_gradual, (HEADS,), jnp.float32, math.log(0.05 / SEQUENCE_SPAN), math.log(0.5 / SEQUENCE_SPAN)))
    fast_rate = jnp.exp(jax.random.uniform(seed_quick, (HEADS,), jnp.float32, math.log(0.02), math.log(0.05)))
    picked = jax.random.randint(seed_selection, (HEADS,), 0, 2) == 0
    fading_rate = jnp.where(picked, fast_rate, slow_rate)
    jagged_perturbation = jnp.exp(jax.random.uniform(seed_jagged, (HEADS, SEQUENCE_SPAN), jnp.float32, -0.7, 0.7))
    spike_present = jax.random.randint(seed_spike, (SEQUENCE_SPAN,), 0, max(SEQUENCE_SPAN // 2, 1)) == 0
    spike_magnitude = jnp.where(spike_present, jax.random.uniform(seed_extent, (SEQUENCE_SPAN,), jnp.float32, 0.2, 0.5), 0.0)
    return -(fading_rate[:, None] * jagged_perturbation) - spike_magnitude[None, :]


def draw_starts(key, part):
    folded = jax.random.fold_in(key, 11)
    seed_which, seed_lottery, seed_planted = jax.random.split(folded, 3)
    quarter = SEQUENCE_SPAN // 4
    which_end = jax.random.randint(seed_which, (), 0, 2)
    region_first = which_end * (SEQUENCE_SPAN - quarter)
    position = jnp.arange(SEQUENCE_SPAN, dtype=jnp.int32)
    within_region = (position >= region_first) & (position < region_first + quarter)
    lottery = jax.random.randint(seed_lottery, (SEQUENCE_SPAN,), 0, TOK_DEV) == 0
    planted = region_first + jax.random.randint(seed_planted, (), 0, quarter)
    return jnp.where(within_region & lottery | (position == planted), 1, 0).astype(jnp.int32)


def level_of(own_key, dims, pieces, least, high):
    loudness = 1.0
    for dim, parts in pieces:
        steps = jax.random.uniform(jax.random.fold_in(jax.random.fold_in(own_key, 6), dim), (parts,), jnp.float32, least / len(pieces), high / len(pieces))
        loudness = loudness * jnp.repeat(jnp.exp(steps), dims[dim] // parts).reshape((-1,) + (1,) * (len(dims) - 1 - dim))
    return loudness


def normal_values(own_key, dims, scale, reach, cuts=(), kind=jnp.bfloat16):
    entries = scale * jax.random.normal(own_key, dims, jnp.float32)
    if cuts:
        entries = entries * level_of(own_key, dims, cuts, -0.22, 0.18)
    return jnp.clip(entries, -reach, reach).astype(kind)


def setup_inputs(seed: int = 0) -> dict:
    splits = jax.random.split(jax.random.key(seed), 11)
    features = normal_values(splits[0], (SEQUENCE_SPAN, INNER), 1.0, 6.0, ((0, 8), (1, 4)))
    gate_values = normal_values(splits[1], (SEQUENCE_SPAN, INNER), 1.0, 6.0, ((0, 8), (1, 4)))
    write_proj = normal_values(splits[2], (SEQUENCE_SPAN, GROUPS * NSTATE), (1.0 / (NSTATE * TOK_DEV) ** 0.5), 0.0234375, ((0, 8), (1, 4)))
    read_proj = normal_values(splits[3], (SEQUENCE_SPAN, GROUPS * NSTATE), 1.0, 6.0, ((0, 8), (1, 4)))
    step_size = jnp.clip(jnp.exp(math.log(2.0) - 2.0794415 * jax.random.uniform(splits[4], (HEADS, SEQUENCE_SPAN), jnp.float32) ** level_of(splits[4], (HEADS, SEQUENCE_SPAN), ((0, 4), (1, 8)), -0.2, 0.2)), 0.25, 2.0)
    log_decay = draw_log_decay(jax.random.fold_in(splits[10], 71), 0)
    starts = draw_starts(jax.random.fold_in(splits[10], 71), 0)
    skip_weight = jnp.clip(0.5 + 1.0 * jax.random.uniform(splits[7], (HEADS,), jnp.float32) ** level_of(splits[7], (HEADS,), ((0, 4),), -0.2, 0.2), 0.5, 1.5)
    norm_gain = jnp.clip(1.0 + 0.18 * jax.random.normal(splits[8], (INNER,), jnp.float32), 0.1, 1.9)
    out_weight = normal_values(splits[9], (INNER, D), INNER ** -0.5, 0.0625, ((0, 4),))
    return dict(features=features, gate_values=gate_values, write_proj=write_proj, read_proj=read_proj, step_size=step_size, log_decay=log_decay, starts=starts, skip_weight=skip_weight, norm_gain=norm_gain, out_weight=out_weight)


eps = 1e-05

def reference(features, gate_values, write_proj, read_proj, step_size, log_decay, starts, skip_weight, norm_gain, out_weight):
    blocks = SEQUENCE_SPAN // SPAN
    per_group = HEADS // GROUPS
    feat_all = features.reshape(blocks, SPAN, HEADS, HEAD_DIM)
    gate_all = gate_values.reshape(blocks, SPAN, INNER)
    write_all = write_proj.reshape(blocks, SPAN, GROUPS, NSTATE)
    read_all = read_proj.reshape(blocks, SPAN, GROUPS, NSTATE)
    step_all = step_size.reshape(HEADS, blocks, SPAN).transpose(1, 0, 2)
    decay_all = log_decay.reshape(HEADS, blocks, SPAN).transpose(1, 0, 2)
    start_all = starts.reshape(blocks, SPAN)
    position = jnp.arange(SPAN)
    causal = position[:, None] >= position[None, :]

    def advance(hidden_state, inputs):
        feat_blk, gate_blk, write_blk, read_blk, step_blk, decay_blk, start_blk = inputs
        running = jnp.cumsum(decay_blk, axis=1)
        seg_local = jnp.cumsum(start_blk)
        together = (seg_local[:, None] == seg_local[None, :]) & causal
        spread_log = running[:, :, None] - running[:, None, :]
        damping = jnp.where(together[None], jnp.exp(jnp.where(together[None], spread_log, 0.0)), 0.0)
        scores = jnp.einsum('ign,jgn->gij', read_blk.astype(jnp.float32), write_blk.astype(jnp.float32))
        weights = ((damping * step_blk[:, None, :]).reshape(GROUPS, per_group, SPAN, SPAN) * scores[:, None]).astype(jnp.bfloat16)
        weights = weights.reshape(HEADS, SPAN, SPAN)
        intra_out = jnp.einsum('hij,jhp->ihp', weights.astype(jnp.float32), feat_blk.astype(jnp.float32))
        entry_read = lax.optimization_barrier(hidden_state.astype(jnp.bfloat16)).astype(jnp.float32)
        carried_out = jnp.einsum('ign,gepn->igep', read_blk.astype(jnp.float32), entry_read.reshape(GROUPS, per_group, HEAD_DIM, NSTATE)).reshape(SPAN, HEADS, HEAD_DIM)
        reach_scale = jnp.where(seg_local[None, :] == 0, jnp.exp(running), 0.0).T
        mixed_out = intra_out + reach_scale[:, :, None] * carried_out + skip_weight[None, :, None] * feat_blk.astype(jnp.float32)
        gated = mixed_out.reshape(SPAN, INNER) * jax.nn.silu(gate_blk.astype(jnp.float32))
        grouped = gated.reshape(SPAN, GROUPS, INNER // GROUPS)
        mean_square = lax.optimization_barrier(jnp.mean(grouped * grouped, axis=-1, keepdims=True))
        normed = ((grouped * lax.rsqrt(mean_square + eps)).reshape(SPAN, INNER) * norm_gain[None, :]).astype(jnp.bfloat16)
        block_out = jnp.dot(normed, out_weight, preferred_element_type=jnp.float32).astype(jnp.bfloat16)
        tail_scale = jnp.where(seg_local[None, :] == seg_local[-1], jnp.exp(running[:, -1:] - running), 0.0) * step_blk
        scaled_in = (tail_scale.T[:, :, None] * feat_blk.astype(jnp.float32)).astype(jnp.bfloat16)
        block_state = jnp.einsum('jgep,jgn->gepn', scaled_in.astype(jnp.float32).reshape(SPAN, GROUPS, per_group, HEAD_DIM), write_blk.astype(jnp.float32)).reshape(HEADS, HEAD_DIM, NSTATE)
        keep_scale = jnp.where(seg_local[-1] == 0, jnp.exp(running[:, -1]), 0.0)
        hidden_state = keep_scale[:, None, None] * hidden_state + block_state
        return (hidden_state, block_out)
    initial = jnp.zeros((HEADS, HEAD_DIM, NSTATE), jnp.float32)
    final_state, outputs = lax.scan(advance, initial, (feat_all, gate_all, write_all, read_all, step_all, decay_all, start_all))
    return outputs.reshape(SEQUENCE_SPAN, D)
```

```python
import jax
import jax.numpy as jnp
import numpy as np
from jax import lax
from jax.experimental import pallas as pl
from jax.experimental.pallas import tpu as pltpu
from jax.sharding import PartitionSpec as P

HEADS = 128
HEAD_DIM = 64
NSTATE = 128
GROUPS = 8
SPAN = 256
KROWS = 8
LOG2E = 1.4426950408889634
VMEM = 48 * 1024 * 1024

eps = 1e-05
F32 = jnp.float32
BF16 = jnp.bfloat16


def three_parts(value, axis):
    high = value.astype(BF16)
    rest = value - high.astype(F32)
    middle = rest.astype(BF16)
    low = (rest - middle.astype(F32)).astype(BF16)
    return jnp.concatenate([high, middle, low], axis=axis)


def head_spread(heads, channels):
    row = lax.broadcasted_iota(jnp.int32, (3 * heads, channels), 0)
    col = lax.broadcasted_iota(jnp.int32, (3 * heads, channels), 1)
    return jnp.where(lax.rem(row, heads) == lax.div(col, HEAD_DIM), 1.0, 0.0).astype(BF16)


def dot(a, b, contract=((1,), (0,))):
    return lax.dot_general(a, b, (contract, ((), ())), preferred_element_type=F32)


def states_kernel(me, feat, write, step, decay, starts, *refs, per_group, blocks, groups, pieces, width):
    msgs = refs[:pieces]
    pre_s, pre_k, vrow, segrow, cols, stack, run_s, run_k = refs[pieces:]
    group, block = pl.program_id(0), pl.program_id(1)
    upper = lax.broadcasted_iota(jnp.int32, (SPAN, SPAN), 0) <= lax.broadcasted_iota(
        jnp.int32, (SPAN, SPAN), 1
    )
    upper = jnp.where(upper, 1.0, 0.0).astype(BF16)
    begins = jnp.broadcast_to(starts[...].astype(F32), (16, SPAN)).astype(BF16)
    sums = dot(jnp.concatenate([three_parts(decay[...], 0), begins], axis=0), upper)
    cum = sums[:per_group] + sums[per_group : 2 * per_group] + sums[2 * per_group : 3 * per_group]
    seg = sums[3 * per_group : 3 * per_group + 8]
    dt = step[...]
    seg_row = seg[0:1]
    seg_last = seg_row[:, SPAN - 1 :]
    last = cum[:, SPAN - 1 :]
    tail = jnp.where(seg_row == seg_last, jnp.exp(last - cum), 0.0) * dt
    keep = jnp.where(seg_last == 0.0, jnp.exp(last), 0.0)
    spread = head_spread(per_group, feat.shape[1])
    tail_all = dot(three_parts(tail, 0), spread, ((0,), (0,)))
    scaled = (tail_all * feat[...].astype(F32)).astype(BF16)
    state = dot(write[...], scaled, ((0,), (0,)))
    keep_all = dot(three_parts(jnp.broadcast_to(keep, (per_group, 128)), 0), spread, ((0,), (0,)))
    keep_all = keep_all[:KROWS]

    reach = jnp.where(seg_row == 0.0, jnp.exp(cum), 0.0)
    vrow[...] = cum * LOG2E - jnp.log2(dt)
    segrow[...] = seg
    fill = jnp.zeros((128 - 2 * per_group - 8, SPAN), F32)
    cols[0] = jnp.concatenate([cum * LOG2E, reach, seg, fill], axis=0).T

    @pl.when(block == 0)
    def _():
        run_s[...] = state
        run_k[...] = keep_all

    @pl.when(block > 0)
    def _():
        run_s[...] = keep_all[0:1] * run_s[...] + state
        run_k[...] = keep_all * run_k[...]

    @pl.when(block < blocks - 1)
    def _():
        pre_s[0] = run_s[...]
        pre_k[0] = run_k[...]

    @pl.when(block == blocks - 1)
    def _():
        here = pieces // groups
        for index in range(here):
            part = slice(index * width, (index + 1) * width)
            stack[group * here + index, :NSTATE] = run_s[:, part]
            stack[group * here + index, NSTATE:] = run_k[:, part]

    @pl.when((block == blocks - 1) & (group == groups - 1))
    def _():
        for offset in range(pieces):
            msgs[offset][...] = stack[me[0] ^ offset]


def states_call(me, features, write_proj, step_size, log_decay, starts, pieces):
    tokens, channels = features.shape
    heads = step_size.shape[0]
    groups = write_proj.shape[1] // NSTATE
    blocks = tokens // SPAN
    per_group, gch = heads // groups, channels // groups
    width = channels // pieces
    last = blocks - 2

    def kernel(*refs):
        states_kernel(
            *refs, per_group=per_group, blocks=blocks, groups=groups, pieces=pieces, width=width
        )

    outs = pl.pallas_call(
        kernel,
        grid_spec=pltpu.PrefetchScalarGridSpec(
            num_scalar_prefetch=1,
            grid=(groups, blocks),
            in_specs=[
                pl.BlockSpec((SPAN, gch), lambda g, b, m: (b, g)),
                pl.BlockSpec((SPAN, NSTATE), lambda g, b, m: (b, g)),
                pl.BlockSpec((per_group, SPAN), lambda g, b, m: (g, b)),
                pl.BlockSpec((per_group, SPAN), lambda g, b, m: (g, b)),
                pl.BlockSpec((1, SPAN), lambda g, b, m: (0, b)),
            ],
            out_specs=[pl.BlockSpec((NSTATE + KROWS, width), lambda g, b, m: (0, 0))] * pieces
            + [
                pl.BlockSpec((1, NSTATE, gch), lambda g, b, m: (jnp.minimum(b, last), 0, g)),
                pl.BlockSpec((1, KROWS, gch), lambda g, b, m: (jnp.minimum(b, last), 0, g)),
                pl.BlockSpec((per_group, SPAN), lambda g, b, m: (g, b)),
                pl.BlockSpec((8, SPAN), lambda g, b, m: (0, b)),
                pl.BlockSpec((1, SPAN, 128), lambda g, b, m: (g, b, 0)),
            ],
            scratch_shapes=[
                pltpu.VMEM((pieces, NSTATE + KROWS, width), F32),
                pltpu.VMEM((NSTATE, gch), F32),
                pltpu.VMEM((KROWS, gch), F32),
            ],
        ),
        out_shape=[jax.ShapeDtypeStruct((NSTATE + KROWS, width), F32)] * pieces
        + [
            jax.ShapeDtypeStruct((blocks - 1, NSTATE, channels), F32),
            jax.ShapeDtypeStruct((blocks - 1, KROWS, channels), F32),
            jax.ShapeDtypeStruct((heads, tokens), F32),
            jax.ShapeDtypeStruct((8, tokens), F32),
            jax.ShapeDtypeStruct((groups, tokens, 128), F32),
        ],
        compiler_params=pltpu.CompilerParams(vmem_limit_bytes=VMEM),
        name="states",
    )(me, features, write_proj, step_size, log_decay, starts.reshape(1, tokens))
    return outs[:pieces], outs[pieces:]


def intra_kernel(feat, write, read, vrow, segrow, cols, skip, out, *, per_group):
    half = SPAN // 2
    x = feat[...]
    scores = dot(read[...], write[...], ((1,), (1,)))
    row = lax.broadcasted_iota(jnp.int32, (SPAN, SPAN), 0)
    col = lax.broadcasted_iota(jnp.int32, (SPAN, SPAN), 1)
    seg_i = cols[0, :, 2 * per_group : 2 * per_group + 1]
    together = (seg_i == segrow[0:1]) & (row >= col)
    scores = jnp.where(together, scores, 0.0)
    lane = lax.broadcasted_iota(jnp.int32, (SPAN, 2 * HEAD_DIM), 1)
    for pair in range(per_group // 2):
        part = slice(pair * 2 * HEAD_DIM, (pair + 1) * 2 * HEAD_DIM)
        xp = x[:, part]
        top = skip[:, part] * xp[:half].astype(F32)
        low = skip[:, part] * xp[half:].astype(F32)
        for which in range(2):
            head = 2 * pair + which
            mine = (lane >= HEAD_DIM) if which else (lane < HEAD_DIM)
            xh = jnp.where(mine, xp, jnp.zeros_like(xp))
            ci = cols[0, :, head : head + 1]
            vj = vrow[head : head + 1, :]
            w_top = jnp.exp2(jnp.minimum(ci[:half] - vj[:, :half], 1.0)) * scores[:half, :half]
            w_low = jnp.exp2(jnp.minimum(ci[half:] - vj, 1.0)) * scores[half:]
            top = top + dot(w_top.astype(BF16), xh[:half])
            low = low + dot(w_low.astype(BF16), xh)
        out[:half, part] = top
        out[half:, part] = low


def intra_call(group, features, write_proj, read_proj, vrow, segrow, cols, skip_row):
    tokens, channels = features.shape
    groups = write_proj.shape[1] // NSTATE
    per_group, gch = vrow.shape[0] // groups, channels // groups
    blocks = tokens // SPAN

    def kernel(*refs):
        intra_kernel(*refs, per_group=per_group)

    return pl.pallas_call(
        kernel,
        grid=(blocks,),
        in_specs=[
            pl.BlockSpec((SPAN, gch), lambda b: (b, group)),
            pl.BlockSpec((SPAN, NSTATE), lambda b: (b, group)),
            pl.BlockSpec((SPAN, NSTATE), lambda b: (b, group)),
            pl.BlockSpec((per_group, SPAN), lambda b: (group, b)),
            pl.BlockSpec((8, SPAN), lambda b: (0, b)),
            pl.BlockSpec((1, SPAN, 128), lambda b: (group, b, 0)),
            pl.BlockSpec((1, gch), lambda b: (0, group)),
        ],
        out_specs=pl.BlockSpec((SPAN, gch), lambda b: (b, 0)),
        out_shape=jax.ShapeDtypeStruct((tokens, gch), F32),
        compiler_params=pltpu.CompilerParams(vmem_limit_bytes=VMEM),
        cost_estimate=pl.CostEstimate(
            flops=8 * 10**9, bytes_accessed=tokens * gch * 6, transcendentals=0
        ),
        name="intra",
    )(features, write_proj, read_proj, vrow, segrow, cols, skip_row)


def prefix_kernel(me, *refs, pieces):
    ins, outs, stack = refs[:pieces], refs[pieces : 2 * pieces], refs[2 * pieces]
    for offset in range(pieces):
        stack[me[0] ^ offset] = ins[offset][...]
    entry = jnp.zeros(outs[0].shape, F32)
    for device in range(pieces):
        state, keep = stack[device, :NSTATE], stack[device, NSTATE : NSTATE + 1]
        stack[device, :NSTATE] = entry
        entry = keep * entry + state
    for offset in range(pieces):
        outs[offset][...] = stack[me[0] ^ offset, :NSTATE]


def prefix_call(me, parts):
    pieces, width = len(parts), parts[0].shape[1]

    def kernel(*refs):
        prefix_kernel(*refs, pieces=pieces)

    return pl.pallas_call(
        kernel,
        grid_spec=pltpu.PrefetchScalarGridSpec(
            num_scalar_prefetch=1,
            grid=(1,),
            in_specs=[pl.BlockSpec((NSTATE + KROWS, width), lambda i, m: (0, 0))] * pieces,
            out_specs=[pl.BlockSpec((NSTATE, width), lambda i, m: (0, 0))] * pieces,
            scratch_shapes=[pltpu.VMEM((pieces, NSTATE + KROWS, width), F32)],
        ),
        out_shape=[jax.ShapeDtypeStruct((NSTATE, width), F32)] * pieces,
        compiler_params=pltpu.CompilerParams(vmem_limit_bytes=VMEM),
        name="prefix",
    )(me, *parts)


def exchange(parts, axis):
    count = len(parts)
    return [parts[0]] + [
        lax.ppermute(parts[offset], axis, [(i, i ^ offset) for i in range(count)])
        for offset in range(1, count)
    ]


def relay(parts, axis):
    count = lax.axis_size(axis)
    total = parts[0][:NSTATE]
    keep = parts[0][NSTATE : NSTATE + 1]
    steps = [(i, i + 1) for i in range(count - 1)]

    def step(index, incoming):
        return lax.ppermute(keep * incoming + total, axis, steps)

    return [lax.fori_loop(0, count - 1, step, jnp.zeros_like(total))]


def normed_kernel(me, order, *refs, pieces, groups, rows, per_group):
    entries = refs[:pieces]
    pre_s, pre_k = refs[pieces : pieces + 2]
    inner = refs[pieces + 2 : pieces + 2 + groups]
    gate, read, cols, gain, out, held = refs[pieces + 2 + groups :]
    width = entries[0].shape[1]
    blocks = held.shape[0]

    @pl.when(pl.program_id(0) == 0)
    def _():
        for offset in range(pieces):
            piece = me[0] ^ offset
            entry = entries[offset][...]
            held[0, piece] = entry.astype(BF16)
            part = pl.ds(pl.multiple_of(piece * width, 128), width)
            for block in range(1, blocks):
                held[block, piece] = (
                    pre_k[block - 1, 0:1, part] * entry + pre_s[block - 1, :, part]
                ).astype(BF16)

    chunk = order[pl.program_id(0)]
    block = lax.div(chunk * rows, SPAN)
    gch = inner[0].shape[1]
    here = pieces // groups if pieces >= groups else 0
    spread = head_spread(per_group, gch)
    for group in range(groups):
        part = slice(group * gch, (group + 1) * gch)
        c_rows = read[:, group * NSTATE : (group + 1) * NSTATE]
        reach = dot(three_parts(cols[group, :, per_group : 2 * per_group], 1), spread)
        if here:
            carried = jnp.concatenate(
                [dot(c_rows, held[block, group * here + k]) for k in range(here)], axis=1
            )
        else:
            carried = dot(c_rows, held[block, 0, :, part])
        y = inner[group][...] + reach * carried
        g = gate[:, part].astype(F32)
        gated = y * (g / (1.0 + jnp.exp(-g)))
        mean_square = jnp.mean(gated * gated, axis=1, keepdims=True)
        out[0, :, part] = (gated * lax.rsqrt(mean_square + eps) * gain[:, part]).astype(BF16)


def normed_call(me, order, entries, pre_s, pre_k, inner, gate_values, read_proj, cols, gain):
    tokens, channels = gate_values.shape
    groups, pieces, width = len(inner), len(entries), entries[0].shape[1]
    count = order.shape[0]
    rows = tokens // count
    blocks = tokens // SPAN
    per_group = channels // groups // HEAD_DIM

    def kernel(*refs):
        normed_kernel(*refs, pieces=pieces, groups=groups, rows=rows, per_group=per_group)

    def whole(value):
        zeros = (0,) * value.ndim
        return pl.BlockSpec(value.shape, lambda j, m, o: zeros)

    def chunk(columns):
        return pl.BlockSpec((rows, columns), lambda j, m, o: (o[j], 0))

    return pl.pallas_call(
        kernel,
        grid_spec=pltpu.PrefetchScalarGridSpec(
            num_scalar_prefetch=2,
            grid=(count,),
            in_specs=[whole(e) for e in entries]
            + [whole(pre_s), whole(pre_k)]
            + [chunk(channels // groups)] * groups
            + [
                chunk(channels),
                chunk(groups * NSTATE),
                pl.BlockSpec((groups, rows, 128), lambda j, m, o: (0, o[j], 0)),
                whole(gain),
            ],
            out_specs=pl.BlockSpec((1, rows, channels), lambda j, m, o: (j, 0, 0)),
            scratch_shapes=[pltpu.VMEM((blocks, pieces, NSTATE, width), BF16)],
        ),
        out_shape=jax.ShapeDtypeStruct((count, rows, channels), BF16),
        compiler_params=pltpu.CompilerParams(vmem_limit_bytes=VMEM),
        name="normed",
    )(me, order, *entries, pre_s, pre_k, *inner, gate_values, read_proj, cols, gain)


def project_call(normed, out_weight, chunks, first, columns):
    _, rows, channels = normed.shape
    tile = min(512, columns)
    start = first // tile

    def kernel(a, w, out):
        out[...] = dot(a[...].reshape(chunks * rows, channels), w[...]).reshape(out.shape)

    return pl.pallas_call(
        kernel,
        grid=(columns // tile,),
        in_specs=[
            pl.BlockSpec((chunks, rows, channels), lambda j: (0, 0, 0)),
            pl.BlockSpec((channels, tile), lambda j: (0, start + j)),
        ],
        out_specs=pl.BlockSpec((chunks, rows, tile), lambda j: (0, 0, j)),
        out_shape=jax.ShapeDtypeStruct((chunks, rows, columns), F32),
        compiler_params=pltpu.CompilerParams(vmem_limit_bytes=VMEM),
        cost_estimate=pl.CostEstimate(
            flops=2 * chunks * rows * channels * columns,
            bytes_accessed=2 * channels * columns + 4 * chunks * rows * columns,
            transcendentals=0,
        ),
        name="project",
    )(normed, out_weight)


def line_tables(count):
    order, up, down = [], np.zeros((count, count), np.int32), np.zeros((count, count), np.int32)
    for me in range(count):
        def step(c):
            return count - c + me if c > me else (count + c - me if c < me else 10 * count)

        order.append(sorted(range(count), key=lambda c: (step(c), abs(c - me))))
        for s in range(1, count):
            if me < count - 1 and s > me:
                up[me, s] = order[me].index(count - s + me)
            if me > 0 and s > count - 1 - me:
                down[me, s] = order[me].index(s - count + me)
    return np.array(order, np.int32), up, down


def add_call(sel, mine, up, down, piece, final):
    count, rows, columns = mine.shape
    width = up.shape[1]
    tile = min(1024, width)
    tiles = width // tile
    moving = pl.BlockSpec((rows, tile), lambda j, s: (0, j))

    def own(place):
        return pl.BlockSpec((1, rows, tile), lambda j, s: (place(s), 0, piece * tiles + j))

    if final:
        def kernel(sel, a, c, d, out):
            out[...] = (a[0] + c[...] + d[...]).astype(BF16)

        return pl.pallas_call(
            kernel,
            grid_spec=pltpu.PrefetchScalarGridSpec(
                num_scalar_prefetch=1,
                grid=(tiles,),
                in_specs=[own(lambda s: count - 1), moving, moving],
                out_specs=moving,
            ),
            out_shape=jax.ShapeDtypeStruct((rows, width), BF16),
            name="last_sum",
        )(sel, mine, up, down)

    def kernel(sel, a, b, c, d, out_up, out_down):
        out_up[...] = a[0] + c[...]
        out_down[...] = b[0] + d[...]

    return pl.pallas_call(
        kernel,
        grid_spec=pltpu.PrefetchScalarGridSpec(
            num_scalar_prefetch=1,
            grid=(tiles,),
            in_specs=[own(lambda s: s[0]), own(lambda s: s[1]), moving, moving],
            out_specs=[moving, moving],
        ),
        out_shape=[jax.ShapeDtypeStruct((rows, width), F32)] * 2,
        cost_estimate=pl.CostEstimate(
            flops=10**10, bytes_accessed=24 * rows * width, transcendentals=0
        ),
        name="sum",
    )(sel, mine, mine, up, down)


def line_sum(first, mine, up_table, down_table, axis):
    count, me = lax.axis_size(axis), lax.axis_index(axis)
    ups, downs = jnp.asarray(up_table)[me], jnp.asarray(down_table)[me]
    pieces = len(first)
    up, down = [None] * pieces, [None] * pieces
    for s in range(1, count):
        sel = jnp.stack([ups[s], downs[s]])
        for p in range(pieces):
            if s == 1:
                to_up = to_down = first[p]
            else:
                to_up, to_down = add_call(sel, mine, up[p], down[p], p, False)
            up[p] = lax.ppermute(to_up, axis, [(i, i + 1) for i in range(count - 1) if s > i])
            down[p] = lax.ppermute(
                to_down, axis, [(i, i - 1) for i in range(1, count) if s > count - 1 - i]
            )
    sel = jnp.stack([ups[0], downs[0]])
    return jnp.concatenate(
        [add_call(sel, mine, up[p], down[p], p, True) for p in range(pieces)], axis=1
    )


def body(
    features,
    gate_values,
    write_proj,
    read_proj,
    step_size,
    log_decay,
    starts,
    skip_weight,
    norm_gain,
    out_weight,
):
    channels = features.shape[1]
    groups = write_proj.shape[1] // NSTATE
    count = lax.axis_size("ctx")
    direct = channels % (128 * count) == 0 and count & (count - 1) == 0 and count % groups == 0
    me = lax.axis_index("ctx").astype(jnp.int32).reshape(1) if direct else jnp.zeros((1,), jnp.int32)
    msgs, (pre_s, pre_k, vrow, segrow, cols) = states_call(
        me, features, write_proj, step_size, log_decay, starts, count if direct else groups
    )
    if direct:
        entries = exchange(prefix_call(me, exchange(msgs, "ctx")), "ctx")
    else:
        entries = [relay([m], "ctx")[0] for m in msgs]
    skip_row = jnp.repeat(skip_weight, HEAD_DIM).reshape(1, channels)
    inner = [
        intra_call(g, features, write_proj, read_proj, vrow, segrow, cols, skip_row)
        for g in range(groups)
    ]
    order, up_table, down_table = line_tables(lax.axis_size("head"))
    normed = normed_call(
        me,
        jnp.asarray(order)[lax.axis_index("head")],
        entries,
        pre_s,
        pre_k,
        inner,
        gate_values,
        read_proj,
        cols,
        norm_gain.reshape(1, channels),
    )
    wide = out_weight.shape[1]
    pieces = 4
    first = [
        project_call(normed, out_weight, 1, p * wide // pieces, wide // pieces)[0]
        for p in range(pieces)
    ]
    mine = project_call(normed, out_weight, order.shape[0], 0, wide)
    return line_sum(first, mine, up_table, down_table, "head")


def solution(mesh):
    placed = (
        P("ctx", "head"),
        P("ctx", "head"),
        P("ctx", "head"),
        P("ctx", "head"),
        P("head", "ctx"),
        P("head", "ctx"),
        P("ctx"),
        P("head"),
        P("head"),
        P("head", None),
    )
    return jax.shard_map(
        body, mesh=mesh, in_specs=placed, out_specs=P(("ctx", "head"), None), check_vma=False
    )
```

```python
import jax
import jax.numpy as jnp
import numpy as np
from jax import lax
from jax.experimental import pallas as pl
from jax.experimental.pallas import tpu as pltpu
from jax.sharding import PartitionSpec as P

HEADS = 128
HEAD_DIM = 64
NSTATE = 128
GROUPS = 8
SPAN = 256
KROWS = 8
LOG2E = 1.4426950408889634
MIB = 1024 * 1024

eps = 1e-05
F32 = jnp.float32
BF16 = jnp.bfloat16


def three_parts(value, axis):
    high = value.astype(BF16)
    rest = value - high.astype(F32)
    middle = rest.astype(BF16)
    low = (rest - middle.astype(F32)).astype(BF16)
    return jnp.concatenate([high, middle, low], axis=axis)


def head_spread(heads, channels):
    row = lax.broadcasted_iota(jnp.int32, (3 * heads, channels), 0)
    col = lax.broadcasted_iota(jnp.int32, (3 * heads, channels), 1)
    return jnp.where(lax.rem(row, heads) == lax.div(col, HEAD_DIM), 1.0, 0.0).astype(BF16)


def dot(a, b, contract=((1,), (0,))):
    return lax.dot_general(a, b, (contract, ((), ())), preferred_element_type=F32)


def block_sums(decay, starts):
    heads = decay.shape[0]
    row = lax.broadcasted_iota(jnp.int32, (SPAN, SPAN), 0)
    col = lax.broadcasted_iota(jnp.int32, (SPAN, SPAN), 1)
    upper = jnp.where(row <= col, 1.0, 0.0).astype(BF16)
    begins = jnp.broadcast_to(starts.astype(F32), (16, SPAN)).astype(BF16)
    sums = dot(jnp.concatenate([three_parts(decay, 0), begins], axis=0), upper)
    cum = sums[:heads] + sums[heads : 2 * heads] + sums[2 * heads : 3 * heads]
    return cum, sums[3 * heads : 3 * heads + 8]


def position(direct):
    if not direct:
        return 0, 0
    me = lax.axis_index("ctx").astype(jnp.int32)
    return lax.rem(me, 2), lax.div(me, 2)


def params(mib):
    return pltpu.CompilerParams(vmem_limit_bytes=mib * MIB)


def states_call(direct, features, write_proj, step_size, log_decay, starts, pieces):
    tokens, channels = features.shape
    heads = step_size.shape[0]
    groups = write_proj.shape[1] // NSTATE
    blocks = tokens // SPAN
    per_group, gch = heads // groups, channels // groups
    width = channels // (2 * pieces)

    def kernel(
        feat_hbm, write_hbm, step_hbm, decay_hbm, starts_hbm, mine, other, pre,
        feat, write, step, decay, starts, total, sems, small_sems,
    ):
        small = [
            pltpu.make_async_copy(src, dst, small_sems.at[k])
            for k, (src, dst) in enumerate(
                [(decay_hbm, decay), (starts_hbm, starts), (step_hbm, step), (write_hbm, write)]
            )
        ]
        for copy in small:
            copy.start()
        copies = []
        for group in range(groups):
            for block in range(blocks):
                copy = pltpu.make_async_copy(
                    feat_hbm.at[pl.ds(block * SPAN, SPAN), pl.ds(group * gch, gch)],
                    feat.at[block, group],
                    sems.at[block, group],
                )
                copy.start()
                copies.append(copy)
        for copy in small[:3]:
            copy.wait()
        spread = head_spread(per_group, gch)
        scales = []
        for block in range(blocks):
            span = slice(block * SPAN, (block + 1) * SPAN)
            cum, seg = block_sums(decay[:, span], starts[:, span])
            seg_last, last = seg[0:1, SPAN - 1 :], cum[:, SPAN - 1 :]
            tail = jnp.where(seg[0:1] == seg_last, jnp.exp(last - cum), 0.0) * step[:, span]
            keep = jnp.where(seg_last == 0.0, jnp.exp(last), 0.0)
            scales.append((tail, jnp.broadcast_to(keep, (heads, 128))))
        small[3].wait()
        for group in range(groups):
            rows = slice(group * per_group, (group + 1) * per_group)
            part = slice(group * gch, (group + 1) * gch)
            for block in range(blocks):
                span = slice(block * SPAN, (block + 1) * SPAN)
                tail, keep = scales[block]
                tail = dot(three_parts(tail[rows], 0), spread, ((0,), (0,)))
                keep = dot(three_parts(keep[rows], 0), spread, ((0,), (0,)))[:KROWS]
                copies[group * blocks + block].wait()
                scaled = (tail * feat[block, group].astype(F32)).astype(BF16)
                state = dot(
                    write[span, group * NSTATE : (group + 1) * NSTATE], scaled, ((0,), (0,))
                )
                if block > 0:
                    state = keep[0:1] * total[:NSTATE, part] + state
                    keep = keep * total[NSTATE:, part]
                total[:NSTATE, part] = state
                total[NSTATE:, part] = keep
                if block < blocks - 1:
                    pre[block, :NSTATE, part] = state
                    pre[block, NSTATE:, part] = keep
        core, _ = position(direct)
        for piece in range(pieces):
            here = (core * pieces + piece) * width
            there = ((1 - core) * pieces + piece) * width
            mine[piece] = total[:, pl.ds(pl.multiple_of(here, 128), width)]
            other[piece] = total[:, pl.ds(pl.multiple_of(there, 128), width)]

    half = jax.ShapeDtypeStruct((pieces, NSTATE + KROWS, width), F32)
    vmem = pl.BlockSpec(memory_space=pltpu.VMEM)
    return pl.pallas_call(
        kernel,
        in_specs=[pl.BlockSpec(memory_space=pltpu.HBM)] * 5,
        out_specs=[vmem] * 3,
        scratch_shapes=[
            pltpu.VMEM((blocks, groups, SPAN, gch), BF16),
            pltpu.VMEM(write_proj.shape, BF16),
            pltpu.VMEM(step_size.shape, F32),
            pltpu.VMEM(log_decay.shape, F32),
            pltpu.VMEM((1, tokens), jnp.int32),
            pltpu.VMEM((NSTATE + KROWS, channels), F32),
            pltpu.SemaphoreType.DMA((blocks, groups)),
            pltpu.SemaphoreType.DMA((4,)),
        ],
        out_shape=[half, half, jax.ShapeDtypeStruct((blocks - 1, NSTATE + KROWS, channels), F32)],
        compiler_params=params(60),
        name="states",
    )(features, write_proj, step_size, log_decay, starts.reshape(1, tokens))


def intra_call(group, features, write_proj, read_proj, step_size, log_decay, starts, skip_weight, after):
    tokens, channels = features.shape
    heads = step_size.shape[0]
    groups = write_proj.shape[1] // NSTATE
    per_group, gch = heads // groups, channels // groups
    blocks = tokens // SPAN
    half = SPAN // 2

    def kernel(feat, write, read, step, decay, starts, skip, after, out, reach):
        cum, seg = block_sums(decay[...], starts[...])
        cum_log2 = cum * LOG2E
        vrow = cum_log2 - jnp.log2(step[...])
        far = jnp.where(seg[0:1] == 0.0, jnp.exp(cum), 0.0)
        fill = jnp.zeros((128 - 2 * per_group - 8, SPAN), F32)
        cols = jnp.concatenate([far, cum_log2, seg, fill], axis=0).T
        reach[...] = cols
        x = feat[...]
        scores = dot(read[...], write[...], ((1,), (1,)))
        row = lax.broadcasted_iota(jnp.int32, (SPAN, SPAN), 0)
        col = lax.broadcasted_iota(jnp.int32, (SPAN, SPAN), 1)
        together = (cols[:, 2 * per_group : 2 * per_group + 1] == seg[0:1]) & (row >= col)
        scores = jnp.where(together, scores, 0.0)
        own = jnp.broadcast_to(skip[:, group * per_group : (group + 1) * per_group], (8, per_group))
        skip_row = dot(three_parts(own, 1), head_spread(per_group, gch))[0:1]
        lane = lax.broadcasted_iota(jnp.int32, (SPAN, 2 * HEAD_DIM), 1)
        for pair in range(per_group // 2):
            part = slice(pair * 2 * HEAD_DIM, (pair + 1) * 2 * HEAD_DIM)
            xp = x[:, part]
            top = skip_row[:, part] * xp[:half].astype(F32)
            low = skip_row[:, part] * xp[half:].astype(F32)
            for which in range(2):
                head = 2 * pair + which
                mine = (lane >= HEAD_DIM) if which else (lane < HEAD_DIM)
                xh = jnp.where(mine, xp, jnp.zeros_like(xp))
                ci = cols[:, per_group + head : per_group + head + 1]
                vj = vrow[head : head + 1, :]
                w_top = jnp.exp2(jnp.minimum(ci[:half] - vj[:, :half], 1.0)) * scores[:half, :half]
                w_low = jnp.exp2(jnp.minimum(ci[half:] - vj, 1.0)) * scores[half:]
                top = top + dot(w_top.astype(BF16), xh[:half])
                low = low + dot(w_low.astype(BF16), xh)
            out[:half, part] = top
            out[half:, part] = low

    return pl.pallas_call(
        kernel,
        grid=(blocks,),
        in_specs=[
            pl.BlockSpec((SPAN, gch), lambda b: (b, group)),
            pl.BlockSpec((SPAN, NSTATE), lambda b: (b, group)),
            pl.BlockSpec((SPAN, NSTATE), lambda b: (b, group)),
            pl.BlockSpec((per_group, SPAN), lambda b: (group, b)),
            pl.BlockSpec((per_group, SPAN), lambda b: (group, b)),
            pl.BlockSpec((1, SPAN), lambda b: (0, b)),
            pl.BlockSpec((1, heads), lambda b: (0, 0)),
            pl.BlockSpec(memory_space=pl.ANY),
        ],
        out_specs=[
            pl.BlockSpec((SPAN, gch), lambda b: (b, 0)),
            pl.BlockSpec((SPAN, 128), lambda b: (b, 0)),
        ],
        out_shape=[
            jax.ShapeDtypeStruct((tokens, gch), F32),
            jax.ShapeDtypeStruct((tokens, 128), F32),
        ],
        compiler_params=params(12),
        cost_estimate=pl.CostEstimate(flops=10**9, bytes_accessed=10**6, transcendentals=0),
        name="intra",
    )(
        features,
        write_proj,
        read_proj,
        step_size,
        log_decay,
        starts.reshape(1, tokens),
        skip_weight.reshape(1, heads),
        after,
    )


def chip_call(mine, theirs):
    pieces, rows, width = mine.shape

    def kernel(mine, theirs, *outs):
        core, chip = position(True)
        first_core = core == 0
        for offset in range(pieces):
            piece = chip ^ offset
            a, b = mine[piece], theirs[piece]
            first, second = jnp.where(first_core, a, b), jnp.where(first_core, b, a)
            keep = second[NSTATE:]
            outs[offset][:NSTATE] = keep[0:1] * first[:NSTATE] + second[:NSTATE]
            outs[offset][NSTATE:] = keep * first[NSTATE:]

    vmem = pl.BlockSpec(memory_space=pltpu.VMEM)
    return pl.pallas_call(
        kernel,
        in_specs=[vmem, vmem],
        out_specs=[vmem] * pieces,
        out_shape=[jax.ShapeDtypeStruct((rows, width), F32)] * pieces,
        compiler_params=params(6),
        name="chip_states",
    )(mine, theirs)


def prefix_call(parts, after):
    pieces, (rows, width) = len(parts), parts[0].shape

    def kernel(*refs):
        _, chip_here = position(True)
        ins, outs, stack = refs[:pieces], refs[pieces + 1 : 2 * pieces + 1], refs[2 * pieces + 1]
        for offset in range(pieces):
            stack[chip_here ^ offset] = ins[offset][...]
        entry = jnp.zeros((NSTATE, width), F32)
        for chip in range(pieces):
            state, keep = stack[chip, :NSTATE], stack[chip, NSTATE : NSTATE + 1]
            stack[chip, :NSTATE] = entry
            entry = keep * entry + state
        for offset in range(pieces):
            outs[offset][...] = stack[chip_here ^ offset, :NSTATE]

    vmem = pl.BlockSpec(memory_space=pltpu.VMEM)
    return pl.pallas_call(
        kernel,
        in_specs=[vmem] * pieces + [pl.BlockSpec(memory_space=pl.ANY)],
        out_specs=[vmem] * pieces,
        scratch_shapes=[pltpu.VMEM((pieces, rows, width), F32)],
        out_shape=[jax.ShapeDtypeStruct((NSTATE, width), F32)] * pieces,
        compiler_params=params(4),
        name="prefix",
    )(*parts, after)


def fold_call(theirs, pre, tokens):
    channels = pre.shape[2]
    blocks = tokens // SPAN
    parts, _, width = theirs[0].shape if theirs else (1, 0, channels // 2)

    def kernel(*refs):
        their_refs, (pre, out) = refs[:-2], refs[-2:]
        core, _ = position(bool(theirs))
        for side in range(2):
            for index in range(parts):
                piece = (core if side == 0 else 1 - core) * parts + index
                part = pl.ds(pl.multiple_of(piece * width, 128), width)
                state = jnp.zeros((NSTATE, width), F32)
                keep = jnp.ones((KROWS, width), F32)
                if theirs:
                    before = their_refs[side][index]
                    state = jnp.where(core == 0, state, before[:NSTATE])
                    keep = jnp.where(core == 0, keep, before[NSTATE:])
                out[0, :NSTATE, part] = state
                out[0, NSTATE:, part] = keep
                for block in range(1, blocks):
                    mult = pre[block - 1, NSTATE:, part]
                    out[block, :NSTATE, part] = mult[0:1] * state + pre[block - 1, :NSTATE, part]
                    out[block, NSTATE:, part] = mult * keep

    vmem = pl.BlockSpec(memory_space=pltpu.VMEM)
    return pl.pallas_call(
        kernel,
        in_specs=[vmem] * (len(theirs) + 1),
        out_specs=vmem,
        out_shape=jax.ShapeDtypeStruct((blocks, NSTATE + KROWS, channels), F32),
        compiler_params=params(8),
        name="fold",
    )(*theirs, pre)


def exchange(parts, axis):
    count = lax.axis_size(axis)
    return [parts[0]] + [
        lax.ppermute(parts[k], axis, [(i, i ^ (2 * k)) for i in range(count)])
        for k in range(1, len(parts))
    ]


def over(value, axis):
    return lax.ppermute(value, axis, [(i, i ^ 1) for i in range(lax.axis_size(axis))])


def chain(total, axis):
    count = lax.axis_size(axis)
    state, keep = total[:, :NSTATE], total[:, NSTATE : NSTATE + 1]
    steps = [(i, i + 1) for i in range(count - 1)]

    def step(index, incoming):
        return lax.ppermute(keep * incoming + state, axis, steps)

    return lax.fori_loop(0, count - 1, step, jnp.zeros_like(state))


def chunk_normed(blk, held, inner, reach, gate, read, gain):
    groups = len(inner)
    gch = inner[0].shape[1]
    per_group = gch // HEAD_DIM
    pieces, width = held.shape[1], held.shape[3]
    here = pieces // groups
    spread = head_spread(per_group, gch)
    result = []
    for group in range(groups):
        part = slice(group * gch, (group + 1) * gch)
        c_rows = read[:, group * NSTATE : (group + 1) * NSTATE]
        far = dot(three_parts(reach[group][:, :per_group], 1), spread)
        carried = [dot(c_rows, held[blk, group * here + k]) for k in range(here)]
        y = inner[group][...] + far * (jnp.concatenate(carried, axis=1) if here > 1 else carried[0])
        g = gate[:, part].astype(F32)
        gated = y * (g / (1.0 + jnp.exp(-g)))
        mean_square = jnp.mean(gated * gated, axis=1, keepdims=True)
        result.append((gated * lax.rsqrt(mean_square + eps) * gain[:, part]).astype(BF16))
    return result


def hold_entries(scal, entries, fold, held, blk, slot):
    parts = len(entries) // 2
    width = held.shape[-1]
    for k, ref in enumerate(entries):
        half = scal[0] if k < parts else 1 - scal[0]
        piece = half * parts + (scal[1] ^ (k % parts))
        part = pl.ds(pl.multiple_of(piece * width, 128), width)
        entry = ref[...].reshape(NSTATE, width)
        held[slot, piece] = (
            fold[blk, NSTATE : NSTATE + 1, part] * entry + fold[blk, :NSTATE, part]
        ).astype(BF16)


def first_call(scal, entries, fold, inner, reach, gate, read, gain, out_weight, rows, columns, early):
    tokens, channels = gate.shape
    groups, pieces, width = len(inner), len(entries), entries[0].shape[-1]
    tile = min(512, columns)
    total = early * columns

    def kernel(scal, *refs):
        entries, refs = refs[:pieces], refs[pieces:]
        inner, reach, refs = refs[:groups], refs[groups : 2 * groups], refs[2 * groups :]
        fold, gate_hbm, read, gain, w_hbm, out, *firsts, weight, gate, held, sems, gate_sem = refs
        gate_copy = pltpu.make_async_copy(
            gate_hbm.at[pl.ds(pl.multiple_of(scal[2] * rows, rows), rows)], gate, gate_sem
        )
        gate_copy.start()
        copies = []
        for t in range(total // tile):
            cut = pl.ds(t * tile, tile)
            copy = pltpu.make_async_copy(w_hbm.at[:, cut], weight.at[:, cut], sems.at[t])
            copy.start()
            copies.append(copy)
        hold_entries(scal, entries, fold, held, 0, 0)
        gate_copy.wait()
        normed = jnp.concatenate(chunk_normed(0, held, inner, reach, gate, read, gain), axis=1)
        out[0] = normed
        for t in range(total // tile):
            cut = slice(t * tile, (t + 1) * tile)
            copies[t].wait()
            at = t * tile % columns
            firsts[t * tile // columns][0, :, at : at + tile] = dot(normed, weight[:, cut])

    def whole(value):
        zeros = (0,) * value.ndim
        return pl.BlockSpec(value.shape, lambda j, s: zeros)

    def chunk(size):
        return pl.BlockSpec((rows, size), lambda j, s: (s[2], 0))

    return pl.pallas_call(
        kernel,
        grid_spec=pltpu.PrefetchScalarGridSpec(
            num_scalar_prefetch=1,
            grid=(1,),
            in_specs=[whole(v) for v in entries]
            + [chunk(channels // groups)] * groups
            + [chunk(128)] * groups
            + [
                pl.BlockSpec(
                    (1, NSTATE + KROWS, channels), lambda j, s: (lax.div(s[2] * rows, SPAN), 0, 0)
                ),
                pl.BlockSpec(memory_space=pltpu.HBM),
                chunk(groups * NSTATE),
                whole(gain),
                pl.BlockSpec(memory_space=pltpu.HBM),
            ],
            out_specs=[
                pl.BlockSpec((1, rows, channels), lambda j, s: (0, 0, 0)),
            ]
            + [pl.BlockSpec((1, rows, columns), lambda j, s: (0, 0, 0))] * early,
            scratch_shapes=[
                pltpu.VMEM((channels, total), BF16),
                pltpu.VMEM((rows, channels), BF16),
                pltpu.VMEM((1, pieces, NSTATE, width), BF16),
                pltpu.SemaphoreType.DMA((total // tile,)),
                pltpu.SemaphoreType.DMA(()),
            ],
        ),
        out_shape=[
            jax.ShapeDtypeStruct((1, rows, channels), BF16),
        ]
        + [jax.ShapeDtypeStruct((1, rows, columns), F32)] * early,
        compiler_params=params(34),
        name="first",
    )(scal, *entries, *inner, *reach, fold, gate, read, gain, out_weight)


def rest_call(scal, entries, fold, inner, reach, gate, read, gain, rows):
    tokens, channels = gate.shape
    groups, pieces, width = len(inner), len(entries), entries[0].shape[-1]
    count, blocks = tokens // rows, tokens // SPAN
    gch = channels // groups

    def kernel(scal, *refs):
        entries, refs = refs[:pieces], refs[pieces:]
        inner, reach, refs = refs[:groups], refs[groups : 2 * groups], refs[2 * groups :]
        fold, gate_hbm, read, gain, out, gate, held, sems = refs
        step = pl.program_id(0)

        def gate_copy(k):
            first_row = pl.multiple_of(scal[3 + k] * rows, rows)
            return pltpu.make_async_copy(gate_hbm.at[pl.ds(first_row, rows)], gate.at[k], sems.at[k])

        @pl.when(step == 0)
        def _():
            for k in range(count - 1):
                gate_copy(k).start()
            for block in range(blocks):
                hold_entries(scal, entries, fold, held, block, block)

        gate_copy(step).wait()
        blk = lax.div(scal[3 + step] * rows, SPAN)
        now = chunk_normed(blk, held, inner, reach, gate.at[step], read, gain)
        for group, part in enumerate(now):
            out[0, :, group * gch : (group + 1) * gch] = part

    def whole(value):
        zeros = (0,) * value.ndim
        return pl.BlockSpec(value.shape, lambda j, s: zeros)

    def chunk(size):
        return pl.BlockSpec((rows, size), lambda j, s: (s[3 + j], 0))

    return pl.pallas_call(
        kernel,
        grid_spec=pltpu.PrefetchScalarGridSpec(
            num_scalar_prefetch=1,
            grid=(count - 1,),
            in_specs=[whole(v) for v in entries]
            + [chunk(gch)] * groups
            + [chunk(128)] * groups
            + [whole(fold), pl.BlockSpec(memory_space=pltpu.HBM)]
            + [chunk(groups * NSTATE), whole(gain)],
            out_specs=pl.BlockSpec((1, rows, channels), lambda j, s: (j, 0, 0)),
            scratch_shapes=[
                pltpu.VMEM((count - 1, rows, channels), BF16),
                pltpu.VMEM((blocks, pieces, NSTATE, width), BF16),
                pltpu.SemaphoreType.DMA((count - 1,)),
            ],
        ),
        out_shape=jax.ShapeDtypeStruct((count - 1, rows, channels), BF16),
        compiler_params=params(14),
        cost_estimate=pl.CostEstimate(flops=10**9, bytes_accessed=10**6, transcendentals=0),
        name="rest",
    )(scal, *entries, *inner, *reach, fold, gate, read, gain)


def project_call(parts, out_weight, start, columns):
    chunks, rows, channels = sum(p.shape[0] for p in parts), *parts[0].shape[1:]
    tile = min(512, columns)
    tiles = columns // tile

    def kernel(*refs):
        w_hbm, out, weight, sems = refs[len(parts) :]
        copies = []
        for t in range(tiles):
            copy = pltpu.make_async_copy(
                w_hbm.at[:, pl.ds(start + t * tile, tile)], weight.at[t], sems.at[t]
            )
            copy.start()
            copies.append(copy)
        for t in range(tiles):
            copies[t].wait()
            at = 0
            for part in refs[: len(parts)]:
                size = part.shape[0]
                product = dot(part[...].reshape(size * rows, channels), weight[t])
                out[at : at + size, :, t * tile : (t + 1) * tile] = product.reshape(size, rows, tile)
                at += size

    vmem = pl.BlockSpec(memory_space=pltpu.VMEM)
    return pl.pallas_call(
        kernel,
        in_specs=[vmem] * len(parts) + [pl.BlockSpec(memory_space=pltpu.HBM)],
        out_specs=vmem,
        out_shape=jax.ShapeDtypeStruct((chunks, rows, columns), F32),
        scratch_shapes=[
            pltpu.VMEM((tiles, channels, tile), BF16),
            pltpu.SemaphoreType.DMA((tiles,)),
        ],
        compiler_params=params(14),
        cost_estimate=pl.CostEstimate(
            flops=2 * chunks * rows * channels * columns,
            bytes_accessed=2 * channels * columns + 4 * chunks * rows * columns,
            transcendentals=0,
        ),
        name="project",
    )(*parts, out_weight)


def line_tables(count):
    order, up, down = [], np.zeros((count, count), np.int32), np.zeros((count, count), np.int32)
    for me in range(count):
        def step(c):
            return count - c + me if c > me else (count + c - me if c < me else 10 * count)

        order.append(sorted(range(count), key=lambda c: (step(c), abs(c - me))))
        for s in range(1, count):
            if me < count - 1 and s > me:
                up[me, s] = order[me].index(count - s + me)
            if me > 0 and s > count - 1 - me:
                down[me, s] = order[me].index(s - count + me)
    return np.concatenate([np.array(order, np.int32), up, down], axis=1)


def sum_call(scal, mine, up, down, step):
    count, rows, width = mine.shape
    tile = min(1024, width)
    moving = pl.BlockSpec((1, rows, tile), lambda j, s: (0, 0, j))
    at_up, at_down = 2 + count + step, 2 + 2 * count + step

    def kernel(scal, a, b, c, d, out_up, out_down):
        out_up[...] = a[...] + c[...]
        out_down[...] = b[...] + d[...]

    return pl.pallas_call(
        kernel,
        grid_spec=pltpu.PrefetchScalarGridSpec(
            num_scalar_prefetch=1,
            grid=(width // tile,),
            in_specs=[
                pl.BlockSpec((1, rows, tile), lambda j, s: (s[at_up], 0, j)),
                pl.BlockSpec((1, rows, tile), lambda j, s: (s[at_down], 0, j)),
                moving,
                moving,
            ],
            out_specs=[moving, moving],
        ),
        out_shape=[jax.ShapeDtypeStruct(up.shape, F32)] * 2,
        cost_estimate=pl.CostEstimate(
            flops=10**10, bytes_accessed=24 * rows * width, transcendentals=0
        ),
        compiler_params=params(8),
        name="sum",
    )(scal, mine, mine, up, down)


def last_call(so_far, mine, up, down, first, wide):
    count, rows, width = mine.shape
    tile = min(512, width)
    moving = pl.BlockSpec((1, rows, tile), lambda j: (0, 0, j))

    def kernel(a, c, d, *refs):
        refs[-1][...] = (a[0] + c[0] + d[0]).astype(BF16)

    more = [] if so_far is None else [so_far]
    return pl.pallas_call(
        kernel,
        grid=(width // tile,),
        in_specs=[pl.BlockSpec((1, rows, tile), lambda j: (count - 1, 0, j)), moving, moving]
        + [pl.BlockSpec(memory_space=pl.ANY)] * len(more),
        out_specs=pl.BlockSpec((rows, tile), lambda j: (0, first // tile + j)),
        out_shape=jax.ShapeDtypeStruct((rows, wide), BF16),
        input_output_aliases={3: 0} if more else {},
        compiler_params=params(4),
        name="last_sum",
    )(mine, up, down, *more)


def send(to_up, to_down, step, axis):
    count = lax.axis_size(axis)
    return (
        lax.ppermute(to_up, axis, [(i, i + 1) for i in range(count - 1) if step > i]),
        lax.ppermute(to_down, axis, [(i, i - 1) for i in range(1, count) if step > count - 1 - i]),
    )


def body(
    features,
    gate_values,
    write_proj,
    read_proj,
    step_size,
    log_decay,
    starts,
    skip_weight,
    norm_gain,
    out_weight,
):
    tokens, channels = features.shape
    groups = write_proj.shape[1] // NSTATE
    count = lax.axis_size("ctx")
    chips = count // 2
    direct = channels % (128 * count) == 0 and chips & (chips - 1) == 0 and count % groups == 0
    me = lax.axis_index("ctx").astype(jnp.int32)
    place = jnp.stack([me % 2, me // 2]) if direct else jnp.zeros((2,), jnp.int32)
    line = lax.axis_size("head")
    scal = jnp.concatenate([place, jnp.asarray(line_tables(line))[lax.axis_index("head")]])
    rows = tokens // line

    features, scal = lax.optimization_barrier((features, scal))
    mine, other, pre = states_call(
        direct, features, write_proj, step_size, log_decay, starts, chips if direct else 1
    )
    def intra(group, after):
        return intra_call(
            group, features, write_proj, read_proj, step_size, log_decay, starts, skip_weight, after
        )

    if direct:
        theirs = over(other, "ctx")
        totals = chip_call(mine, theirs)
        rest_theirs = lax.ppermute(mine, "ctx", [(i, i + 1) for i in range(0, count, 2)])
        moved = exchange(totals, "ctx")
        local = [intra(0, totals[0])]
        entries = prefix_call(moved, local[0][1])
        own = exchange(entries, "ctx")
        local += [intra(g, entries[0]) for g in range(1, groups)]
        fold = fold_call([theirs, rest_theirs], pre, tokens)
        own, local, fold = lax.optimization_barrier((own, local, fold))
        entries = own + [over(e, "ctx") for e in own]
    else:
        entries = [chain(mine, "ctx"), chain(other, "ctx")]
        local = [intra(g, mine) for g in range(groups)]
        fold = fold_call([], pre, tokens)
    inner, reach = zip(*local)
    rest = (inner, reach, gate_values, read_proj, norm_gain.reshape(1, channels))
    wide = out_weight.shape[1]
    pieces = 4
    cut = wide // pieces
    early = pieces
    normed, *firsts = first_call(scal, entries, fold, *rest, out_weight, rows, cut, early)
    moving = [send(f, f, 1, "head") for f in firsts]
    others = rest_call(scal, entries, fold, *rest, rows)
    mine = [project_call([normed, others], out_weight, p * cut, cut) for p in range(pieces)]
    for s in range(2, line):
        for p in range(pieces):
            moving[p] = send(*sum_call(scal, mine[p], *moving[p], s), s, "head")
    result = None
    for p in range(pieces):
        result = last_call(result, mine[p], *moving[p], p * cut, wide)
    return result


def solution(mesh):
    placed = (
        P("ctx", "head"),
        P("ctx", "head"),
        P("ctx", "head"),
        P("ctx", "head"),
        P("head", "ctx"),
        P("head", "ctx"),
        P("ctx"),
        P("head"),
        P("head"),
        P("head", None),
    )
    return jax.shard_map(
        body, mesh=mesh, in_specs=placed, out_specs=P(("ctx", "head"), None), check_vma=False
    )
```

```python
import jax
import jax.numpy as jnp
import numpy as np
from jax import lax
from jax.experimental import pallas as pl
from jax.experimental.pallas import tpu as pltpu
from jax.sharding import PartitionSpec as P

HEADS = 128
HEAD_DIM = 64
NSTATE = 128
GROUPS = 8
SPAN = 256
KROWS = 8
LOG2E = 1.4426950408889634
MIB = 1024 * 1024

eps = 1e-05
F32 = jnp.float32
BF16 = jnp.bfloat16


def three_parts(value, axis):
    high = value.astype(BF16)
    rest = value - high.astype(F32)
    middle = rest.astype(BF16)
    low = (rest - middle.astype(F32)).astype(BF16)
    return jnp.concatenate([high, middle, low], axis=axis)


def head_spread(heads, channels):
    row = lax.broadcasted_iota(jnp.int32, (3 * heads, channels), 0)
    col = lax.broadcasted_iota(jnp.int32, (3 * heads, channels), 1)
    return jnp.where(lax.rem(row, heads) == lax.div(col, HEAD_DIM), 1.0, 0.0).astype(BF16)


def dot(a, b, contract=((1,), (0,))):
    return lax.dot_general(a, b, (contract, ((), ())), preferred_element_type=F32)


def block_sums(decay, starts):
    heads = decay.shape[0]
    row = lax.broadcasted_iota(jnp.int32, (SPAN, SPAN), 0)
    col = lax.broadcasted_iota(jnp.int32, (SPAN, SPAN), 1)
    upper = jnp.where(row <= col, 1.0, 0.0).astype(BF16)
    begins = jnp.broadcast_to(starts.astype(F32), (16, SPAN)).astype(BF16)
    sums = dot(jnp.concatenate([three_parts(decay, 0), begins], axis=0), upper)
    cum = sums[:heads] + sums[heads : 2 * heads] + sums[2 * heads : 3 * heads]
    return cum, sums[3 * heads : 3 * heads + 8]


def position(direct):
    if not direct:
        return 0, 0
    me = lax.axis_index("ctx").astype(jnp.int32)
    return lax.rem(me, 2), lax.div(me, 2)


def cut(start, size, step=128):
    return pl.ds(start if isinstance(start, int) else pl.multiple_of(start, step), size)


def params(mib):
    return pltpu.CompilerParams(vmem_limit_bytes=mib * MIB)


def states_call(side, direct, features, write_proj, step_size, log_decay, starts, pieces, after):
    tokens, channels = features.shape
    groups = write_proj.shape[1] // NSTATE
    blocks = tokens // SPAN
    parts = max(1, groups // 2)
    heads, size = step_size.shape[0] // 2, channels // 2
    per_part, gch = heads // parts, size // parts
    width = size // pieces

    def kernel(
        feat_hbm, write_hbm, step_hbm, decay_hbm, starts_hbm, after, out, pre,
        feat, write, step, decay, starts, total, sems, write_sems, small_sems,
    ):
        core, _ = position(direct)
        half = core if side == 0 else 1 - core
        rows = cut(half * heads, heads, 8)
        small = [
            pltpu.make_async_copy(src, dst, small_sems.at[k])
            for k, (src, dst) in enumerate(
                [(decay_hbm.at[rows], decay), (starts_hbm, starts), (step_hbm.at[rows], step)]
            )
        ]
        for copy in small:
            copy.start()
        copies = []
        for part in range(parts):
            group = half * parts + part if groups > 1 else 0
            copy = pltpu.make_async_copy(
                write_hbm.at[:, cut(group * NSTATE, NSTATE)], write.at[part], write_sems.at[part]
            )
            copy.start()
            copies.append(copy)
            for block in range(blocks):
                copy = pltpu.make_async_copy(
                    feat_hbm.at[
                        pl.ds(block * SPAN, SPAN), cut(half * size + part * gch, gch)
                    ],
                    feat.at[part, block],
                    sems.at[part, block],
                )
                copy.start()
                copies.append(copy)
        spread = head_spread(per_part, gch)
        for copy in small:
            copy.wait()
        scales = []
        for block in range(blocks):
            span = slice(block * SPAN, (block + 1) * SPAN)
            cum, seg = block_sums(decay[:, span], starts[:, span])
            seg_last, last = seg[0:1, SPAN - 1 :], cum[:, SPAN - 1 :]
            tail = jnp.where(seg[0:1] == seg_last, jnp.exp(last - cum), 0.0) * step[:, span]
            keep = jnp.where(seg_last == 0.0, jnp.exp(last), 0.0)
            scales.append((tail, jnp.broadcast_to(keep, (heads, 128))))
        for part in range(parts):
            rows = slice(part * per_part, (part + 1) * per_part)
            lanes = slice(part * gch, (part + 1) * gch)
            copies.pop(0).wait()
            for block in range(blocks):
                tail, keep = scales[block]
                tail = dot(three_parts(tail[rows], 0), spread, ((0,), (0,)))
                keep = dot(three_parts(keep[rows], 0), spread, ((0,), (0,)))[:KROWS]
                copies.pop(0).wait()
                scaled = (tail * feat[part, block].astype(F32)).astype(BF16)
                state = dot(write[part, block * SPAN : (block + 1) * SPAN], scaled, ((0,), (0,)))
                if block > 0:
                    state = keep[0:1] * total[:NSTATE, lanes] + state
                    keep = keep * total[NSTATE:, lanes]
                total[:NSTATE, lanes] = state
                total[NSTATE:, lanes] = keep
                if block < blocks - 1:
                    pre[block, :NSTATE, lanes] = state
                    pre[block, NSTATE:, lanes] = keep
        for piece in range(pieces):
            out[piece] = total[:, piece * width : (piece + 1) * width]

    vmem = pl.BlockSpec(memory_space=pltpu.VMEM)
    return pl.pallas_call(
        kernel,
        in_specs=[pl.BlockSpec(memory_space=pltpu.HBM)] * 5 + [pl.BlockSpec(memory_space=pl.ANY)],
        out_specs=[vmem] * 2,
        scratch_shapes=[
            pltpu.VMEM((parts, blocks, SPAN, gch), BF16),
            pltpu.VMEM((parts, tokens, NSTATE), BF16),
            pltpu.VMEM((heads, tokens), F32),
            pltpu.VMEM((heads, tokens), F32),
            pltpu.VMEM((1, tokens), jnp.int32),
            pltpu.VMEM((NSTATE + KROWS, size), F32),
            pltpu.SemaphoreType.DMA((parts, blocks)),
            pltpu.SemaphoreType.DMA((parts,)),
            pltpu.SemaphoreType.DMA((3,)),
        ],
        out_shape=[
            jax.ShapeDtypeStruct((pieces, NSTATE + KROWS, width), F32),
            jax.ShapeDtypeStruct((blocks - 1, NSTATE + KROWS, size), F32),
        ],
        compiler_params=params(60 if side else 44),
        cost_estimate=pl.CostEstimate(flops=10**8, bytes_accessed=10**6, transcendentals=0),
        name="states",
    )(features, write_proj, step_size, log_decay, starts.reshape(1, tokens), after)


def intra_call(scal, side, features, write_proj, read_proj, step_size, log_decay, starts, skip_weight, after):
    tokens, channels = features.shape
    heads = step_size.shape[0]
    groups = write_proj.shape[1] // NSTATE
    per_group, gch = heads // groups, channels // groups
    blocks = tokens // SPAN
    half = SPAN // 2

    def group(s):
        return s[0] ^ side if groups > 1 else 0

    def kernel(scal, feat, write, read, step, decay, starts, skip, after, out, reach):
        cum, seg = block_sums(decay[...], starts[...])
        cum_log2 = cum * LOG2E
        vrow = cum_log2 - jnp.log2(step[...])
        far = jnp.where(seg[0:1] == 0.0, jnp.exp(cum), 0.0)
        fill = jnp.zeros((128 - 2 * per_group - 8, SPAN), F32)
        cols = jnp.concatenate([far, cum_log2, seg, fill], axis=0).T
        reach[...] = cols
        x = feat[...]
        scores = dot(read[...], write[...], ((1,), (1,)))
        row = lax.broadcasted_iota(jnp.int32, (SPAN, SPAN), 0)
        col = lax.broadcasted_iota(jnp.int32, (SPAN, SPAN), 1)
        together = (cols[:, 2 * per_group : 2 * per_group + 1] == seg[0:1]) & (row >= col)
        scores = jnp.where(together, scores, 0.0)
        own = skip[:, :per_group]
        for other in range(1, groups):
            theirs = skip[:, other * per_group : (other + 1) * per_group]
            own = jnp.where(group(scal) == other, theirs, own)
        own = jnp.broadcast_to(own, (8, per_group))
        skip_row = dot(three_parts(own, 1), head_spread(per_group, gch))[0:1]
        lane = lax.broadcasted_iota(jnp.int32, (SPAN, 2 * HEAD_DIM), 1)
        for pair in range(per_group // 2):
            part = slice(pair * 2 * HEAD_DIM, (pair + 1) * 2 * HEAD_DIM)
            xp = x[:, part]
            top = skip_row[:, part] * xp[:half].astype(F32)
            low = skip_row[:, part] * xp[half:].astype(F32)
            for which in range(2):
                head = 2 * pair + which
                mine = (lane >= HEAD_DIM) if which else (lane < HEAD_DIM)
                xh = jnp.where(mine, xp, jnp.zeros_like(xp))
                ci = cols[:, per_group + head : per_group + head + 1]
                vj = vrow[head : head + 1, :]
                w_top = jnp.exp2(jnp.minimum(ci[:half] - vj[:, :half], 1.0)) * scores[:half, :half]
                w_low = jnp.exp2(jnp.minimum(ci[half:] - vj, 1.0)) * scores[half:]
                top = top + dot(w_top.astype(BF16), xh[:half])
                low = low + dot(w_low.astype(BF16), xh)
            out[:half, part] = top
            out[half:, part] = low

    return pl.pallas_call(
        kernel,
        grid_spec=pltpu.PrefetchScalarGridSpec(
            num_scalar_prefetch=1,
            grid=(blocks,),
            in_specs=[
                pl.BlockSpec((SPAN, gch), lambda b, s: (b, group(s))),
                pl.BlockSpec((SPAN, NSTATE), lambda b, s: (b, group(s))),
                pl.BlockSpec((SPAN, NSTATE), lambda b, s: (b, group(s))),
                pl.BlockSpec((per_group, SPAN), lambda b, s: (group(s), b)),
                pl.BlockSpec((per_group, SPAN), lambda b, s: (group(s), b)),
                pl.BlockSpec((1, SPAN), lambda b, s: (0, b)),
                pl.BlockSpec((1, heads), lambda b, s: (0, 0)),
                pl.BlockSpec(memory_space=pl.ANY),
            ],
            out_specs=[
                pl.BlockSpec((SPAN, gch), lambda b, s: (b, 0)),
                pl.BlockSpec((SPAN, 128), lambda b, s: (b, 0)),
            ],
        ),
        out_shape=[
            jax.ShapeDtypeStruct((tokens, gch), F32),
            jax.ShapeDtypeStruct((tokens, 128), F32),
        ],
        compiler_params=params(12),
        cost_estimate=pl.CostEstimate(flops=10**9, bytes_accessed=10**6, transcendentals=0),
        name="intra",
    )(
        scal,
        features,
        write_proj,
        read_proj,
        step_size,
        log_decay,
        starts.reshape(1, tokens),
        skip_weight.reshape(1, heads),
        after,
    )


def chip_call(mine, theirs):
    pieces, rows, width = mine.shape

    def kernel(mine, theirs, *outs):
        core, chip = position(True)
        first_core = core == 0
        for offset in range(pieces):
            piece = chip ^ offset
            a, b = mine[piece], theirs[piece]
            first, second = jnp.where(first_core, a, b), jnp.where(first_core, b, a)
            keep = second[NSTATE:]
            outs[offset][:NSTATE] = keep[0:1] * first[:NSTATE] + second[:NSTATE]
            outs[offset][NSTATE:] = keep * first[NSTATE:]

    vmem = pl.BlockSpec(memory_space=pltpu.VMEM)
    return pl.pallas_call(
        kernel,
        in_specs=[vmem, vmem],
        out_specs=[vmem] * pieces,
        out_shape=[jax.ShapeDtypeStruct((rows, width), F32)] * pieces,
        compiler_params=params(6),
        name="chip_states",
    )(mine, theirs)


def prefix_call(parts, after):
    pieces, (rows, width) = len(parts), parts[0].shape

    def kernel(*refs):
        _, chip_here = position(True)
        ins, outs, stack = refs[:pieces], refs[pieces + 1 : 2 * pieces + 1], refs[2 * pieces + 1]
        for offset in range(pieces):
            stack[chip_here ^ offset] = ins[offset][...]
        entry = jnp.zeros((NSTATE, width), F32)
        for chip in range(pieces):
            state, keep = stack[chip, :NSTATE], stack[chip, NSTATE : NSTATE + 1]
            stack[chip, :NSTATE] = entry
            entry = keep * entry + state
        for offset in range(pieces):
            outs[offset][...] = stack[chip_here ^ offset, :NSTATE]

    vmem = pl.BlockSpec(memory_space=pltpu.VMEM)
    return pl.pallas_call(
        kernel,
        in_specs=[vmem] * pieces + [pl.BlockSpec(memory_space=pl.ANY)],
        out_specs=[vmem] * pieces,
        scratch_shapes=[pltpu.VMEM((pieces, rows, width), F32)],
        out_shape=[jax.ShapeDtypeStruct((NSTATE, width), F32)] * pieces,
        compiler_params=params(4),
        name="prefix",
    )(*parts, after)


def fold_call(theirs, pre, tokens, at=()):
    size = pre.shape[2]
    blocks = tokens // SPAN

    def kernel(*refs):
        pre, out = refs[-2:]
        state, keep = jnp.zeros((NSTATE, size), F32), jnp.ones((KROWS, size), F32)
        if theirs:
            core, _ = position(True)
            before = refs[0]
            before = jnp.concatenate(
                [before[(*at, p)] for p in range(theirs[0].shape[-3])], axis=1
            )
            state = jnp.where(core == 0, state, before[:NSTATE])
            keep = jnp.where(core == 0, keep, before[NSTATE:])
        out[0, :NSTATE] = state
        out[0, NSTATE:] = keep
        for block in range(1, blocks):
            here = pre[block - 1]
            out[block, :NSTATE] = here[NSTATE : NSTATE + 1] * state + here[:NSTATE]
            out[block, NSTATE:] = here[NSTATE:] * keep

    vmem = pl.BlockSpec(memory_space=pltpu.VMEM)
    return pl.pallas_call(
        kernel,
        in_specs=[vmem] * (len(theirs) + 1),
        out_specs=vmem,
        out_shape=jax.ShapeDtypeStruct((blocks, NSTATE + KROWS, size), F32),
        compiler_params=params(8),
        name="fold",
    )(*theirs, pre)


def pack_call(entries, mine):
    pieces, rows, width = mine.shape

    def kernel(*refs):
        mine, out = refs[-2:]
        for piece in range(pieces):
            out[0, piece, :NSTATE] = refs[piece][...]
            out[0, piece, NSTATE:] = jnp.zeros((rows - NSTATE, width), F32)
            out[1, piece] = mine[piece]

    vmem = pl.BlockSpec(memory_space=pltpu.VMEM)
    return pl.pallas_call(
        kernel,
        in_specs=[vmem] * (pieces + 1),
        out_specs=vmem,
        out_shape=jax.ShapeDtypeStruct((2, *mine.shape), F32),
        compiler_params=params(6),
        name="pack",
    )(*entries, mine)


def exchange(parts, axis):
    count = lax.axis_size(axis)
    return [parts[0]] + [
        lax.ppermute(parts[k], axis, [(i, i ^ (2 * k)) for i in range(count)])
        for k in range(1, len(parts))
    ]


def over(value, axis):
    return lax.ppermute(value, axis, [(i, i ^ 1) for i in range(lax.axis_size(axis))])


def chain(total, axis):
    count = lax.axis_size(axis)
    state, keep = total[:, :NSTATE], total[:, NSTATE : NSTATE + 1]
    steps = [(i, i + 1) for i in range(count - 1)]

    def step(index, incoming):
        return lax.ppermute(keep * incoming + state, axis, steps)

    return lax.fori_loop(0, count - 1, step, jnp.zeros_like(state))


def hold_entries(chip, entries, fold, held):
    pieces, _, width = held.shape
    for offset in range(pieces):
        piece = chip ^ offset
        part = cut(piece * width, width)
        entry = entries[0, offset, :NSTATE]
        held[piece] = (fold[NSTATE : NSTATE + 1, part] * entry + fold[:NSTATE, part]).astype(BF16)


def group_normed(held, c_rows, inner, reach, gate, gain):
    gch = inner.shape[1]
    per_group = gch // HEAD_DIM
    far = dot(three_parts(reach[:, :per_group], 1), head_spread(per_group, gch))
    carried = [dot(c_rows, piece) for piece in held]
    y = inner + far * (jnp.concatenate(carried, axis=1) if len(carried) > 1 else carried[0])
    g = gate.astype(F32)
    gated = y * (g / (1.0 + jnp.exp(-g)))
    mean_square = jnp.mean(gated * gated, axis=1, keepdims=True)
    return (gated * lax.rsqrt(mean_square + eps) * gain).astype(BF16)


def first_call(scal, sides, entries, fold, inner, reach, gate, read, gain, out_weight, rows, columns, early, before):
    tokens, channels = gate.shape
    gch = inner.shape[1]
    groups = channels // gch
    parts, width = entries[0].shape[1], entries[0].shape[3]
    wide = early * columns
    tile = min(512, columns)
    last = groups == 1 or bool(before)

    def group(s):
        return s[0] ^ sides[0] if groups > 1 else 0

    def kernel(scal, *refs):
        entry_refs, refs = refs[: len(sides)], refs[len(sides) :]
        folds, refs = refs[: len(sides)], refs[len(sides) :]
        inner, reach, read, gain, gate_hbm, w_hbm = refs[:6]
        earlier, refs = refs[6 : 6 + len(before)], refs[6 + len(before) :]
        out, *firsts, weight, gate, held, sems, gate_sem = refs
        lanes = cut(group(scal) * gch, gch)
        gate_copy = pltpu.make_async_copy(
            gate_hbm.at[cut(scal[2] * rows, rows, rows), lanes], gate, gate_sem
        )
        gate_copy.start()
        copies = []
        for t in range(wide // tile):
            copy = pltpu.make_async_copy(
                w_hbm.at[cut(group(scal) * gch, gch), pl.ds(t * tile, tile)], weight.at[t], sems.at[t]
            )
            copy.start()
            copies.append(copy)
        for k in range(len(sides)):
            hold_entries(scal[1], entry_refs[k], folds[k].at[0], held.at[k])
        gate_copy.wait()
        pieces = [held[k, p] for k in range(len(sides)) for p in range(parts)]
        normed = group_normed(pieces, read[...], inner[...], reach[...], gate[...], gain[...])
        if last:
            out[0, :, lanes] = normed
            if before:
                out[0, :, cut((1 - group(scal)) * gch, gch)] = earlier[0][...]
        else:
            out[...] = normed
        for t in range(wide // tile):
            copies[t].wait()
            product = dot(normed, weight[t])
            here = slice(t * tile, (t + 1) * tile)
            if not last:
                firsts[0][:, here] = product
                continue
            if before:
                product = product + earlier[1][:, here]
            at = t * tile % columns
            firsts[t * tile // columns][0, :, at : at + tile] = product

    def whole(value):
        zeros = (0,) * value.ndim
        return pl.BlockSpec(value.shape, lambda j, s: zeros)

    def chunk(size):
        return pl.BlockSpec((rows, size), lambda j, s: (s[2], 0))

    if last:
        shapes = [((1, rows, channels), BF16)] + [((1, rows, columns), F32)] * (wide // columns)
    else:
        shapes = [((rows, gch), BF16), ((rows, wide), F32)]
    return pl.pallas_call(
        kernel,
        grid_spec=pltpu.PrefetchScalarGridSpec(
            num_scalar_prefetch=1,
            grid=(1,),
            in_specs=[whole(v) for v in entries]
            + [pl.BlockSpec((1, *f.shape[1:]), lambda j, s: (lax.div(s[2] * rows, SPAN), 0, 0)) for f in fold]
            + [
                chunk(gch),
                chunk(128),
                pl.BlockSpec((rows, NSTATE), lambda j, s: (s[2], group(s))),
                pl.BlockSpec((1, gch), lambda j, s: (0, group(s))),
                pl.BlockSpec(memory_space=pltpu.HBM),
                pl.BlockSpec(memory_space=pltpu.HBM),
            ]
            + [whole(v) for v in before],
            out_specs=[
                pl.BlockSpec(shape, lambda j, s, zeros=(0,) * len(shape): zeros) for shape, _ in shapes
            ],
            scratch_shapes=[
                pltpu.VMEM((wide // tile, gch, tile), BF16),
                pltpu.VMEM((rows, gch), BF16),
                pltpu.VMEM((len(sides), parts, NSTATE, width), BF16),
                pltpu.SemaphoreType.DMA((wide // tile,)),
                pltpu.SemaphoreType.DMA(()),
            ],
        ),
        out_shape=[jax.ShapeDtypeStruct(shape, kind) for shape, kind in shapes],
        compiler_params=params(40),
        name="first",
    )(scal, *entries, *fold, inner, reach, read, gain, gate, out_weight, *before)


def rest_call(scal, entries, fold, inner, reach, gate, read, gain, rows):
    tokens, channels = gate.shape
    groups, parts, width = len(inner), entries[0].shape[1], entries[0].shape[3]
    count, blocks = tokens // rows, tokens // SPAN
    gch = channels // groups

    def kernel(scal, *refs):
        entry_refs, refs = refs[:2], refs[2:]
        inner, reach, refs = refs[:groups], refs[groups : 2 * groups], refs[2 * groups :]
        folds, refs = refs[:2], refs[2:]
        gate_hbm, read, gain, out, gate, held, sems = refs
        step = pl.program_id(0)

        def gate_copy(k):
            first_row = pl.multiple_of(scal[3 + k] * rows, rows)
            return pltpu.make_async_copy(gate_hbm.at[pl.ds(first_row, rows)], gate.at[k], sems.at[k])

        @pl.when(step == 0)
        def _():
            for k in range(count - 1):
                gate_copy(k).start()
            for block in range(blocks):
                for side in range(2):
                    hold_entries(scal[1], entry_refs[side], folds[side].at[block], held.at[block, side])

        gate_copy(step).wait()
        blk = lax.div(scal[3 + step] * rows, SPAN)
        for k in range(groups):
            group = scal[0] ^ k if groups > 1 else 0
            sides = [k] if groups > 1 else [0, 1]
            pieces = [held[blk, side, p] for side in sides for p in range(parts)]
            lanes = cut(group * gch, gch)
            c_rows = read[:, cut(group * NSTATE, NSTATE)]
            out[0, :, lanes] = group_normed(
                pieces, c_rows, inner[k][...], reach[k][...], gate[step, :, lanes], gain[:, lanes]
            )

    def whole(value):
        zeros = (0,) * value.ndim
        return pl.BlockSpec(value.shape, lambda j, s: zeros)

    def chunk(size):
        return pl.BlockSpec((rows, size), lambda j, s: (s[3 + j], 0))

    return pl.pallas_call(
        kernel,
        grid_spec=pltpu.PrefetchScalarGridSpec(
            num_scalar_prefetch=1,
            grid=(count - 1,),
            in_specs=[whole(v) for v in entries]
            + [chunk(gch)] * groups
            + [chunk(128)] * groups
            + [whole(f) for f in fold]
            + [pl.BlockSpec(memory_space=pltpu.HBM)]
            + [chunk(groups * NSTATE), whole(gain)],
            out_specs=pl.BlockSpec((1, rows, channels), lambda j, s: (j, 0, 0)),
            scratch_shapes=[
                pltpu.VMEM((count - 1, rows, channels), BF16),
                pltpu.VMEM((blocks, 2, parts, NSTATE, width), BF16),
                pltpu.SemaphoreType.DMA((count - 1,)),
            ],
        ),
        out_shape=jax.ShapeDtypeStruct((count - 1, rows, channels), BF16),
        compiler_params=params(14),
        cost_estimate=pl.CostEstimate(flops=10**9, bytes_accessed=10**6, transcendentals=0),
        name="rest",
    )(scal, *entries, *inner, *reach, *fold, gate, read, gain)


def project_call(parts, out_weight, start, columns, pieces=1):
    chunks, rows, channels = sum(p.shape[0] for p in parts), *parts[0].shape[1:]
    width = columns // pieces
    tile = min(512, width)
    tiles = columns // tile

    def kernel(*refs):
        w_hbm, *outs, weight, sems = refs[len(parts) :]
        copies = []
        for t in range(tiles):
            copy = pltpu.make_async_copy(
                w_hbm.at[:, pl.ds(start + t * tile, tile)], weight.at[t], sems.at[t]
            )
            copy.start()
            copies.append(copy)
        for t in range(tiles):
            copies[t].wait()
            at = 0
            for part in refs[: len(parts)]:
                size = part.shape[0]
                product = dot(part[...].reshape(size * rows, channels), weight[t])
                out, column = outs[t * tile // width], t * tile % width
                out[at : at + size, :, column : column + tile] = product.reshape(size, rows, tile)
                at += size

    vmem = pl.BlockSpec(memory_space=pltpu.VMEM)
    return pl.pallas_call(
        kernel,
        in_specs=[vmem] * len(parts) + [pl.BlockSpec(memory_space=pltpu.HBM)],
        out_specs=[vmem] * pieces,
        out_shape=[jax.ShapeDtypeStruct((chunks, rows, width), F32)] * pieces,
        scratch_shapes=[
            pltpu.VMEM((tiles, channels, tile), BF16),
            pltpu.SemaphoreType.DMA((tiles,)),
        ],
        compiler_params=params(40),
        cost_estimate=pl.CostEstimate(
            flops=2 * chunks * rows * channels * columns,
            bytes_accessed=2 * channels * columns + 4 * chunks * rows * columns,
            transcendentals=0,
        ),
        name="project",
    )(*parts, out_weight)


def line_tables(count):
    order, up, down = [], np.zeros((count, count), np.int32), np.zeros((count, count), np.int32)
    for me in range(count):
        def step(c):
            return count - c + me if c > me else (count + c - me if c < me else 10 * count)

        order.append(sorted(range(count), key=lambda c: (step(c), abs(c - me))))
        for s in range(1, count):
            if me < count - 1 and s > me:
                up[me, s] = order[me].index(count - s + me)
            if me > 0 and s > count - 1 - me:
                down[me, s] = order[me].index(s - count + me)
    return np.concatenate([np.array(order, np.int32), up, down], axis=1)


def sum_call(scal, mine, up, down, step):
    count, rows, width = mine.shape
    tile = min(1024, width)
    moving = pl.BlockSpec((1, rows, tile), lambda j, s: (0, 0, j))
    at_up, at_down = 2 + count + step, 2 + 2 * count + step

    def kernel(scal, a, b, c, d, out_up, out_down):
        out_up[...] = a[...] + c[...]
        out_down[...] = b[...] + d[...]

    return pl.pallas_call(
        kernel,
        grid_spec=pltpu.PrefetchScalarGridSpec(
            num_scalar_prefetch=1,
            grid=(width // tile,),
            in_specs=[
                pl.BlockSpec((1, rows, tile), lambda j, s: (s[at_up], 0, j)),
                pl.BlockSpec((1, rows, tile), lambda j, s: (s[at_down], 0, j)),
                moving,
                moving,
            ],
            out_specs=[moving, moving],
        ),
        out_shape=[jax.ShapeDtypeStruct(up.shape, F32)] * 2,
        cost_estimate=pl.CostEstimate(
            flops=10**10, bytes_accessed=24 * rows * width, transcendentals=0
        ),
        compiler_params=params(8),
        name="sum",
    )(scal, mine, mine, up, down)


def last_call(so_far, mine, up, down, first, wide):
    count, rows, width = mine.shape
    tile = min(512, width)
    moving = pl.BlockSpec((1, rows, tile), lambda j: (0, 0, j))

    def kernel(a, c, d, *refs):
        refs[-1][...] = (a[0] + c[0] + d[0]).astype(BF16)

    more = [] if so_far is None else [so_far]
    return pl.pallas_call(
        kernel,
        grid=(width // tile,),
        in_specs=[pl.BlockSpec((1, rows, tile), lambda j: (count - 1, 0, j)), moving, moving]
        + [pl.BlockSpec(memory_space=pl.ANY)] * len(more),
        out_specs=pl.BlockSpec((rows, tile), lambda j: (0, first // tile + j)),
        out_shape=jax.ShapeDtypeStruct((rows, wide), BF16),
        input_output_aliases={3: 0} if more else {},
        compiler_params=params(4),
        name="last_sum",
    )(mine, up, down, *more)


def send(to_up, to_down, step, axis):
    count = lax.axis_size(axis)
    return (
        lax.ppermute(to_up, axis, [(i, i + 1) for i in range(count - 1) if step > i]),
        lax.ppermute(to_down, axis, [(i, i - 1) for i in range(1, count) if step > count - 1 - i]),
    )


def body(
    features,
    gate_values,
    write_proj,
    read_proj,
    step_size,
    log_decay,
    starts,
    skip_weight,
    norm_gain,
    out_weight,
):
    tokens, channels = features.shape
    groups = write_proj.shape[1] // NSTATE
    count = lax.axis_size("ctx")
    chips = count // 2
    direct = channels % (128 * count) == 0 and chips & (chips - 1) == 0 and groups == 2
    me = lax.axis_index("ctx").astype(jnp.int32)
    place = jnp.stack([me % 2, me // 2]) if direct else jnp.zeros((2,), jnp.int32)
    line = lax.axis_size("head")
    table = jnp.asarray(line_tables(line))

    def scalars(table):
        return jnp.concatenate([place, table[lax.axis_index("head")]])

    rows = tokens // line

    inputs = (features, write_proj, step_size, log_decay, starts)
    chunks = chips if direct else 1
    other, pre_other = states_call(1, direct, *inputs, chunks, starts)
    mine, pre_mine = states_call(0, direct, *inputs, chunks, other)

    def intra(side, after):
        return intra_call(
            scal, side, features, write_proj, read_proj, step_size, log_decay, starts, skip_weight, after
        )

    if direct:
        theirs = over(other, "ctx")
        totals = chip_call(mine, theirs)
        totals, table = lax.optimization_barrier((totals, table))
        scal = scalars(table)
        moved = exchange(totals, "ctx")
        local = [intra(0, totals[0])]
        entries = prefix_call(moved, local[0][1])
        own = exchange(entries, "ctx")
        local += [intra(g, entries[0]) for g in range(1, groups)]
        fold = [fold_call([theirs], pre_mine, tokens)]
        own, mine, local, fold = lax.optimization_barrier((own, mine, local, fold))
        packed = pack_call(own, mine)
        entries = [packed, over(packed, "ctx")]
        fold.append(fold_call([entries[1]], pre_other, tokens, (1,)))
    else:
        scal = scalars(table)
        entries = [chain(mine, "ctx")[None], chain(other, "ctx")[None]]
        local = [intra(g, mine) for g in range(groups)]
        fold = [fold_call([], pre, tokens) for pre in (pre_mine, pre_other)]
    inner, reach = zip(*local)
    gain = norm_gain.reshape(1, channels)
    wide = out_weight.shape[1]
    pieces = 4
    size = wide // pieces
    early = 2
    firsts = []
    for sides in [[0], [1]] if groups > 1 else [[0, 1]]:
        at = sides[0]
        firsts = first_call(
            scal, sides, [entries[k] for k in sides], [fold[k] for k in sides], inner[at], reach[at], gate_values, read_proj,
            gain, out_weight, rows, size, early, firsts,
        )
    normed, *firsts = firsts
    moving = [send(f, f, 1, "head") for f in firsts]
    late, moving[0] = lax.optimization_barrier((normed, moving[0]))
    firsts = project_call([late], out_weight, early * size, wide - early * size, pieces - early)
    moving += [send(f, f, 1, "head") for f in firsts]
    inner, firsts = lax.optimization_barrier((inner, firsts))
    others = rest_call(scal, entries, fold, inner, reach, gate_values, read_proj, gain, rows)
    mine = [project_call([normed, others], out_weight, p * size, size)[0] for p in range(pieces)]
    sums = None
    for s in range(2, line):
        for p in range(pieces):
            if sums is not None:
                mine[p], sums = lax.optimization_barrier((mine[p], sums))
            sums = sum_call(scal, mine[p], *moving[p], s)
            moving[p] = send(*sums, s, "head")
    result = None
    for p in range(pieces):
        result = last_call(result, mine[p], *moving[p], p * size, wide)
    return result


def solution(mesh):
    placed = (
        P("ctx", "head"),
        P("ctx", "head"),
        P("ctx", "head"),
        P("ctx", "head"),
        P("head", "ctx"),
        P("head", "ctx"),
        P("ctx"),
        P("head"),
        P("head"),
        P("head", None),
    )
    return jax.shard_map(
        body, mesh=mesh, in_specs=placed, out_specs=P(("ctx", "head"), None), check_vma=False
    )
```

```python
import jax
import jax.numpy as jnp
import numpy as np
from jax import lax
from jax.experimental import pallas as pl
from jax.experimental.pallas import tpu as pltpu
from jax.sharding import PartitionSpec as P

HEADS = 128
HEAD_DIM = 64
NSTATE = 128
GROUPS = 8
SPAN = 256
KROWS = 8
LOG2E = 1.4426950408889634
MIB = 1024 * 1024

eps = 1e-05
F32 = jnp.float32
BF16 = jnp.bfloat16


def three_parts(value, axis):
    high = value.astype(BF16)
    rest = value - high.astype(F32)
    middle = rest.astype(BF16)
    low = (rest - middle.astype(F32)).astype(BF16)
    return jnp.concatenate([high, middle, low], axis=axis)


def head_spread(heads, channels):
    row = lax.broadcasted_iota(jnp.int32, (3 * heads, channels), 0)
    col = lax.broadcasted_iota(jnp.int32, (3 * heads, channels), 1)
    return jnp.where(lax.rem(row, heads) == lax.div(col, HEAD_DIM), 1.0, 0.0).astype(BF16)


def dot(a, b, contract=((1,), (0,))):
    return lax.dot_general(a, b, (contract, ((), ())), preferred_element_type=F32)


def block_sums(decay, starts):
    heads = decay.shape[0]
    row = lax.broadcasted_iota(jnp.int32, (SPAN, SPAN), 0)
    col = lax.broadcasted_iota(jnp.int32, (SPAN, SPAN), 1)
    upper = jnp.where(row <= col, 1.0, 0.0).astype(BF16)
    begins = jnp.broadcast_to(starts.astype(F32), (16, SPAN)).astype(BF16)
    sums = dot(jnp.concatenate([three_parts(decay, 0), begins], axis=0), upper)
    cum = sums[:heads] + sums[heads : 2 * heads] + sums[2 * heads : 3 * heads]
    return cum, sums[3 * heads : 3 * heads + 8]


def position(direct):
    if not direct:
        return 0, 0
    me = lax.axis_index("ctx").astype(jnp.int32)
    return lax.rem(me, 2), lax.div(me, 2)


def cut(start, size, step=128):
    return pl.ds(start if isinstance(start, int) else pl.multiple_of(start, step), size)


def params(mib):
    return pltpu.CompilerParams(vmem_limit_bytes=mib * MIB)


def states_call(side, direct, features, write_proj, step_size, log_decay, starts, pieces, after):
    tokens, channels = features.shape
    groups = write_proj.shape[1] // NSTATE
    blocks = tokens // SPAN
    parts = max(1, groups // 2)
    heads, size = step_size.shape[0] // 2, channels // 2
    per_part, gch = heads // parts, size // parts
    width = size // pieces

    def kernel(
        feat_hbm, write_hbm, step_hbm, decay_hbm, starts_hbm, after, out, pre,
        feat, write, step, decay, starts, total, sems, write_sems, small_sems,
    ):
        core, _ = position(direct)
        half = core if side == 0 else 1 - core
        rows = cut(half * heads, heads, 8)
        small = [
            pltpu.make_async_copy(src, dst, small_sems.at[k])
            for k, (src, dst) in enumerate(
                [(decay_hbm.at[rows], decay), (starts_hbm, starts), (step_hbm.at[rows], step)]
            )
        ]
        for copy in small:
            copy.start()
        copies = []
        for part in range(parts):
            group = half * parts + part if groups > 1 else 0
            copy = pltpu.make_async_copy(
                write_hbm.at[:, cut(group * NSTATE, NSTATE)], write.at[part], write_sems.at[part]
            )
            copy.start()
            copies.append(copy)
            for block in range(blocks):
                copy = pltpu.make_async_copy(
                    feat_hbm.at[
                        pl.ds(block * SPAN, SPAN), cut(half * size + part * gch, gch)
                    ],
                    feat.at[part, block],
                    sems.at[part, block],
                )
                copy.start()
                copies.append(copy)
        spread = head_spread(per_part, gch)
        for copy in small:
            copy.wait()
        scales = []
        for block in range(blocks):
            span = slice(block * SPAN, (block + 1) * SPAN)
            cum, seg = block_sums(decay[:, span], starts[:, span])
            seg_last, last = seg[0:1, SPAN - 1 :], cum[:, SPAN - 1 :]
            tail = jnp.where(seg[0:1] == seg_last, jnp.exp(last - cum), 0.0) * step[:, span]
            keep = jnp.where(seg_last == 0.0, jnp.exp(last), 0.0)
            scales.append((tail, jnp.broadcast_to(keep, (heads, 128))))
        for part in range(parts):
            rows = slice(part * per_part, (part + 1) * per_part)
            lanes = slice(part * gch, (part + 1) * gch)
            copies.pop(0).wait()
            for block in range(blocks):
                tail, keep = scales[block]
                tail = dot(three_parts(tail[rows], 0), spread, ((0,), (0,)))
                keep = dot(three_parts(keep[rows], 0), spread, ((0,), (0,)))[:KROWS]
                copies.pop(0).wait()
                scaled = (tail * feat[part, block].astype(F32)).astype(BF16)
                state = dot(write[part, block * SPAN : (block + 1) * SPAN], scaled, ((0,), (0,)))
                if block > 0:
                    state = keep[0:1] * total[:NSTATE, lanes] + state
                    keep = keep * total[NSTATE:, lanes]
                total[:NSTATE, lanes] = state
                total[NSTATE:, lanes] = keep
                if block < blocks - 1:
                    pre[block, :NSTATE, lanes] = state
                    pre[block, NSTATE:, lanes] = keep
        for piece in range(pieces):
            out[piece] = total[:, piece * width : (piece + 1) * width]

    vmem = pl.BlockSpec(memory_space=pltpu.VMEM)
    return pl.pallas_call(
        kernel,
        in_specs=[pl.BlockSpec(memory_space=pltpu.HBM)] * 5 + [pl.BlockSpec(memory_space=pl.ANY)],
        out_specs=[vmem] * 2,
        scratch_shapes=[
            pltpu.VMEM((parts, blocks, SPAN, gch), BF16),
            pltpu.VMEM((parts, tokens, NSTATE), BF16),
            pltpu.VMEM((heads, tokens), F32),
            pltpu.VMEM((heads, tokens), F32),
            pltpu.VMEM((1, tokens), jnp.int32),
            pltpu.VMEM((NSTATE + KROWS, size), F32),
            pltpu.SemaphoreType.DMA((parts, blocks)),
            pltpu.SemaphoreType.DMA((parts,)),
            pltpu.SemaphoreType.DMA((3,)),
        ],
        out_shape=[
            jax.ShapeDtypeStruct((pieces, NSTATE + KROWS, width), F32),
            jax.ShapeDtypeStruct((blocks - 1, NSTATE + KROWS, size), F32),
        ],
        compiler_params=params(60 if side else 44),
        cost_estimate=pl.CostEstimate(flops=10**8, bytes_accessed=10**6, transcendentals=0),
        name="states",
    )(features, write_proj, step_size, log_decay, starts.reshape(1, tokens), after)


def intra_call(scal, side, features, write_proj, read_proj, step_size, log_decay, starts, skip_weight, after):
    tokens, channels = features.shape
    heads = step_size.shape[0]
    groups = write_proj.shape[1] // NSTATE
    per_group, gch = heads // groups, channels // groups
    blocks = tokens // SPAN
    half = SPAN // 2

    def group(s):
        return s[0] ^ side if groups > 1 else 0

    def kernel(scal, feat, write, read, step, decay, starts, skip, after, out, reach):
        cum, seg = block_sums(decay[...], starts[...])
        cum_log2 = cum * LOG2E
        vrow = cum_log2 - jnp.log2(step[...])
        far = jnp.where(seg[0:1] == 0.0, jnp.exp(cum), 0.0)
        fill = jnp.zeros((128 - 2 * per_group - 8, SPAN), F32)
        cols = jnp.concatenate([far, cum_log2, seg, fill], axis=0).T
        reach[...] = cols
        x = feat[...]
        scores = dot(read[...], write[...], ((1,), (1,)))
        row = lax.broadcasted_iota(jnp.int32, (SPAN, SPAN), 0)
        col = lax.broadcasted_iota(jnp.int32, (SPAN, SPAN), 1)
        together = (cols[:, 2 * per_group : 2 * per_group + 1] == seg[0:1]) & (row >= col)
        scores = jnp.where(together, scores, 0.0)
        own = skip[:, :per_group]
        for other in range(1, groups):
            theirs = skip[:, other * per_group : (other + 1) * per_group]
            own = jnp.where(group(scal) == other, theirs, own)
        own = jnp.broadcast_to(own, (8, per_group))
        skip_row = dot(three_parts(own, 1), head_spread(per_group, gch))[0:1]
        lane = lax.broadcasted_iota(jnp.int32, (SPAN, 2 * HEAD_DIM), 1)
        for pair in range(per_group // 2):
            part = slice(pair * 2 * HEAD_DIM, (pair + 1) * 2 * HEAD_DIM)
            xp = x[:, part]
            top = skip_row[:, part] * xp[:half].astype(F32)
            low = skip_row[:, part] * xp[half:].astype(F32)
            for which in range(2):
                head = 2 * pair + which
                mine = (lane >= HEAD_DIM) if which else (lane < HEAD_DIM)
                xh = jnp.where(mine, xp, jnp.zeros_like(xp))
                ci = cols[:, per_group + head : per_group + head + 1]
                vj = vrow[head : head + 1, :]
                w_top = jnp.exp2(jnp.minimum(ci[:half] - vj[:, :half], 1.0)) * scores[:half, :half]
                w_low = jnp.exp2(jnp.minimum(ci[half:] - vj, 1.0)) * scores[half:]
                top = top + dot(w_top.astype(BF16), xh[:half])
                low = low + dot(w_low.astype(BF16), xh)
            out[:half, part] = top
            out[half:, part] = low

    return pl.pallas_call(
        kernel,
        grid_spec=pltpu.PrefetchScalarGridSpec(
            num_scalar_prefetch=1,
            grid=(blocks,),
            in_specs=[
                pl.BlockSpec((SPAN, gch), lambda b, s: (b, group(s))),
                pl.BlockSpec((SPAN, NSTATE), lambda b, s: (b, group(s))),
                pl.BlockSpec((SPAN, NSTATE), lambda b, s: (b, group(s))),
                pl.BlockSpec((per_group, SPAN), lambda b, s: (group(s), b)),
                pl.BlockSpec((per_group, SPAN), lambda b, s: (group(s), b)),
                pl.BlockSpec((1, SPAN), lambda b, s: (0, b)),
                pl.BlockSpec((1, heads), lambda b, s: (0, 0)),
                pl.BlockSpec(memory_space=pl.ANY),
            ],
            out_specs=[
                pl.BlockSpec((SPAN, gch), lambda b, s: (b, 0)),
                pl.BlockSpec((SPAN, 128), lambda b, s: (b, 0)),
            ],
        ),
        out_shape=[
            jax.ShapeDtypeStruct((tokens, gch), F32),
            jax.ShapeDtypeStruct((tokens, 128), F32),
        ],
        compiler_params=params(12),
        cost_estimate=pl.CostEstimate(flops=10**9, bytes_accessed=10**6, transcendentals=0),
        name="intra",
    )(
        scal,
        features,
        write_proj,
        read_proj,
        step_size,
        log_decay,
        starts.reshape(1, tokens),
        skip_weight.reshape(1, heads),
        after,
    )


def chip_call(mine, theirs):
    pieces, rows, width = mine.shape

    def kernel(mine, theirs, *outs):
        core, chip = position(True)
        first_core = core == 0
        for offset in range(pieces):
            piece = chip ^ offset
            a, b = mine[piece], theirs[piece]
            first, second = jnp.where(first_core, a, b), jnp.where(first_core, b, a)
            keep = second[NSTATE:]
            outs[offset][:NSTATE] = keep[0:1] * first[:NSTATE] + second[:NSTATE]
            outs[offset][NSTATE:] = keep * first[NSTATE:]

    vmem = pl.BlockSpec(memory_space=pltpu.VMEM)
    return pl.pallas_call(
        kernel,
        in_specs=[vmem, vmem],
        out_specs=[vmem] * pieces,
        out_shape=[jax.ShapeDtypeStruct((rows, width), F32)] * pieces,
        compiler_params=params(6),
        name="chip_states",
    )(mine, theirs)


def prefix_call(parts, after):
    pieces, (rows, width) = len(parts), parts[0].shape

    def kernel(*refs):
        _, chip_here = position(True)
        ins, outs, stack = refs[:pieces], refs[pieces + 1 : 2 * pieces + 1], refs[2 * pieces + 1]
        for offset in range(pieces):
            stack[chip_here ^ offset] = ins[offset][...]
        entry = jnp.zeros((NSTATE, width), F32)
        for chip in range(pieces):
            state, keep = stack[chip, :NSTATE], stack[chip, NSTATE : NSTATE + 1]
            stack[chip, :NSTATE] = entry
            entry = keep * entry + state
        for offset in range(pieces):
            outs[offset][...] = stack[chip_here ^ offset, :NSTATE]

    vmem = pl.BlockSpec(memory_space=pltpu.VMEM)
    return pl.pallas_call(
        kernel,
        in_specs=[vmem] * pieces + [pl.BlockSpec(memory_space=pl.ANY)],
        out_specs=[vmem] * pieces,
        scratch_shapes=[pltpu.VMEM((pieces, rows, width), F32)],
        out_shape=[jax.ShapeDtypeStruct((NSTATE, width), F32)] * pieces,
        compiler_params=params(4),
        name="prefix",
    )(*parts, after)


def fold_call(theirs, pre, tokens, at=()):
    size = pre.shape[2]
    blocks = tokens // SPAN

    def kernel(*refs):
        pre, out = refs[-2:]
        state, keep = jnp.zeros((NSTATE, size), F32), jnp.ones((KROWS, size), F32)
        if theirs:
            core, _ = position(True)
            before = refs[0]
            before = jnp.concatenate(
                [before[(*at, p)] for p in range(theirs[0].shape[-3])], axis=1
            )
            state = jnp.where(core == 0, state, before[:NSTATE])
            keep = jnp.where(core == 0, keep, before[NSTATE:])
        out[0, :NSTATE] = state
        out[0, NSTATE:] = keep
        for block in range(1, blocks):
            here = pre[block - 1]
            out[block, :NSTATE] = here[NSTATE : NSTATE + 1] * state + here[:NSTATE]
            out[block, NSTATE:] = here[NSTATE:] * keep

    vmem = pl.BlockSpec(memory_space=pltpu.VMEM)
    return pl.pallas_call(
        kernel,
        in_specs=[vmem] * (len(theirs) + 1),
        out_specs=vmem,
        out_shape=jax.ShapeDtypeStruct((blocks, NSTATE + KROWS, size), F32),
        compiler_params=params(8),
        name="fold",
    )(*theirs, pre)


def pack_call(entries, mine):
    pieces, rows, width = mine.shape

    def kernel(*refs):
        mine, out = refs[-2:]
        for piece in range(pieces):
            out[0, piece, :NSTATE] = refs[piece][...]
            out[0, piece, NSTATE:] = jnp.zeros((rows - NSTATE, width), F32)
            out[1, piece] = mine[piece]

    vmem = pl.BlockSpec(memory_space=pltpu.VMEM)
    return pl.pallas_call(
        kernel,
        in_specs=[vmem] * (pieces + 1),
        out_specs=vmem,
        out_shape=jax.ShapeDtypeStruct((2, *mine.shape), F32),
        compiler_params=params(6),
        name="pack",
    )(*entries, mine)


def exchange(parts, axis):
    count = lax.axis_size(axis)
    return [parts[0]] + [
        lax.ppermute(parts[k], axis, [(i, i ^ (2 * k)) for i in range(count)])
        for k in range(1, len(parts))
    ]


def over(value, axis):
    return lax.ppermute(value, axis, [(i, i ^ 1) for i in range(lax.axis_size(axis))])


def chain(total, axis):
    count = lax.axis_size(axis)
    state, keep = total[:, :NSTATE], total[:, NSTATE : NSTATE + 1]
    steps = [(i, i + 1) for i in range(count - 1)]

    def step(index, incoming):
        return lax.ppermute(keep * incoming + state, axis, steps)

    return lax.fori_loop(0, count - 1, step, jnp.zeros_like(state))


def hold_entries(chip, entries, fold, held):
    pieces, _, width = held.shape
    for offset in range(pieces):
        piece = chip ^ offset
        part = cut(piece * width, width)
        entry = entries[0, offset, :NSTATE]
        held[piece] = (fold[NSTATE : NSTATE + 1, part] * entry + fold[:NSTATE, part]).astype(BF16)


def group_normed(held, c_rows, inner, reach, gate, gain):
    gch = inner.shape[1]
    per_group = gch // HEAD_DIM
    far = dot(three_parts(reach[:, :per_group], 1), head_spread(per_group, gch))
    carried = [dot(c_rows, piece) for piece in held]
    y = inner + far * (jnp.concatenate(carried, axis=1) if len(carried) > 1 else carried[0])
    g = gate.astype(F32)
    gated = y * (g / (1.0 + jnp.exp(-g)))
    mean_square = jnp.mean(gated * gated, axis=1, keepdims=True)
    return (gated * lax.rsqrt(mean_square + eps) * gain).astype(BF16)


def first_call(scal, sides, entries, fold, inner, reach, gate, read, gain, out_weight, rows, columns, early, before):
    tokens, channels = gate.shape
    gch = inner.shape[1]
    groups = channels // gch
    parts, width = entries[0].shape[1], entries[0].shape[3]
    wide = early * columns
    tile = min(512, columns)
    last = groups == 1 or bool(before)

    def group(s):
        return s[0] ^ sides[0] if groups > 1 else 0

    def kernel(scal, *refs):
        entry_refs, refs = refs[: len(sides)], refs[len(sides) :]
        folds, refs = refs[: len(sides)], refs[len(sides) :]
        inner, reach, read, gain, gate_hbm, w_hbm = refs[:6]
        earlier, refs = refs[6 : 6 + len(before)], refs[6 + len(before) :]
        out, *firsts, weight, gate, held, sems, gate_sem = refs
        lanes = cut(group(scal) * gch, gch)
        gate_copy = pltpu.make_async_copy(
            gate_hbm.at[cut(scal[2] * rows, rows, rows), lanes], gate, gate_sem
        )
        gate_copy.start()
        copies = []
        for t in range(wide // tile):
            copy = pltpu.make_async_copy(
                w_hbm.at[cut(group(scal) * gch, gch), pl.ds(t * tile, tile)], weight.at[t], sems.at[t]
            )
            copy.start()
            copies.append(copy)
        for k in range(len(sides)):
            hold_entries(scal[1], entry_refs[k], folds[k].at[0], held.at[k])
        gate_copy.wait()
        pieces = [held[k, p] for k in range(len(sides)) for p in range(parts)]
        normed = group_normed(pieces, read[...], inner[...], reach[...], gate[...], gain[...])
        if last:
            out[0, :, lanes] = normed
            if before:
                out[0, :, cut((1 - group(scal)) * gch, gch)] = earlier[0][...]
        else:
            out[...] = normed
        for t in range(wide // tile):
            copies[t].wait()
            product = dot(normed, weight[t])
            here = slice(t * tile, (t + 1) * tile)
            if not last:
                firsts[0][:, here] = product
                continue
            if before:
                product = product + earlier[1][:, here]
            at = t * tile % columns
            firsts[t * tile // columns][0, :, at : at + tile] = product

    def whole(value):
        zeros = (0,) * value.ndim
        return pl.BlockSpec(value.shape, lambda j, s: zeros)

    def chunk(size):
        return pl.BlockSpec((rows, size), lambda j, s: (s[2], 0))

    if last:
        shapes = [((1, rows, channels), BF16)] + [((1, rows, columns), F32)] * (wide // columns)
    else:
        shapes = [((rows, gch), BF16), ((rows, wide), F32)]
    return pl.pallas_call(
        kernel,
        grid_spec=pltpu.PrefetchScalarGridSpec(
            num_scalar_prefetch=1,
            grid=(1,),
            in_specs=[whole(v) for v in entries]
            + [pl.BlockSpec((1, *f.shape[1:]), lambda j, s: (lax.div(s[2] * rows, SPAN), 0, 0)) for f in fold]
            + [
                chunk(gch),
                chunk(128),
                pl.BlockSpec((rows, NSTATE), lambda j, s: (s[2], group(s))),
                pl.BlockSpec((1, gch), lambda j, s: (0, group(s))),
                pl.BlockSpec(memory_space=pltpu.HBM),
                pl.BlockSpec(memory_space=pltpu.HBM),
            ]
            + [whole(v) for v in before],
            out_specs=[
                pl.BlockSpec(shape, lambda j, s, zeros=(0,) * len(shape): zeros) for shape, _ in shapes
            ],
            scratch_shapes=[
                pltpu.VMEM((wide // tile, gch, tile), BF16),
                pltpu.VMEM((rows, gch), BF16),
                pltpu.VMEM((len(sides), parts, NSTATE, width), BF16),
                pltpu.SemaphoreType.DMA((wide // tile,)),
                pltpu.SemaphoreType.DMA(()),
            ],
        ),
        out_shape=[jax.ShapeDtypeStruct(shape, kind) for shape, kind in shapes],
        compiler_params=params(40),
        name="first",
    )(scal, *entries, *fold, inner, reach, read, gain, gate, out_weight, *before)


def rest_call(scal, entries, fold, inner, reach, gate, read, gain, rows):
    tokens, channels = gate.shape
    groups, parts, width = len(inner), entries[0].shape[1], entries[0].shape[3]
    count, blocks = tokens // rows, tokens // SPAN
    gch = channels // groups

    def kernel(scal, *refs):
        entry_refs, refs = refs[:2], refs[2:]
        inner, reach, refs = refs[:groups], refs[groups : 2 * groups], refs[2 * groups :]
        folds, refs = refs[:2], refs[2:]
        gate_hbm, read, gain, out, gate, held, sems = refs
        step = pl.program_id(0)

        def gate_copy(k):
            first_row = pl.multiple_of(scal[3 + k] * rows, rows)
            return pltpu.make_async_copy(gate_hbm.at[pl.ds(first_row, rows)], gate.at[k], sems.at[k])

        @pl.when(step == 0)
        def _():
            for k in range(count - 1):
                gate_copy(k).start()
            for block in range(blocks):
                for side in range(2):
                    hold_entries(scal[1], entry_refs[side], folds[side].at[block], held.at[block, side])

        gate_copy(step).wait()
        blk = lax.div(scal[3 + step] * rows, SPAN)
        for k in range(groups):
            group = scal[0] ^ k if groups > 1 else 0
            sides = [k] if groups > 1 else [0, 1]
            pieces = [held[blk, side, p] for side in sides for p in range(parts)]
            lanes = cut(group * gch, gch)
            c_rows = read[:, cut(group * NSTATE, NSTATE)]
            out[0, :, lanes] = group_normed(
                pieces, c_rows, inner[k][...], reach[k][...], gate[step, :, lanes], gain[:, lanes]
            )

    def whole(value):
        zeros = (0,) * value.ndim
        return pl.BlockSpec(value.shape, lambda j, s: zeros)

    def chunk(size):
        return pl.BlockSpec((rows, size), lambda j, s: (s[3 + j], 0))

    return pl.pallas_call(
        kernel,
        grid_spec=pltpu.PrefetchScalarGridSpec(
            num_scalar_prefetch=1,
            grid=(count - 1,),
            in_specs=[whole(v) for v in entries]
            + [chunk(gch)] * groups
            + [chunk(128)] * groups
            + [whole(f) for f in fold]
            + [pl.BlockSpec(memory_space=pltpu.HBM)]
            + [chunk(groups * NSTATE), whole(gain)],
            out_specs=pl.BlockSpec((1, rows, channels), lambda j, s: (j, 0, 0)),
            scratch_shapes=[
                pltpu.VMEM((count - 1, rows, channels), BF16),
                pltpu.VMEM((blocks, 2, parts, NSTATE, width), BF16),
                pltpu.SemaphoreType.DMA((count - 1,)),
            ],
        ),
        out_shape=jax.ShapeDtypeStruct((count - 1, rows, channels), BF16),
        compiler_params=params(14),
        cost_estimate=pl.CostEstimate(flops=10**9, bytes_accessed=10**6, transcendentals=0),
        name="rest",
    )(scal, *entries, *inner, *reach, *fold, gate, read, gain)


def project_call(parts, out_weight, start, columns, pieces=1):
    chunks, rows, channels = sum(p.shape[0] for p in parts), *parts[0].shape[1:]
    width = columns // pieces
    tile = min(512, width)
    tiles = columns // tile

    def kernel(*refs):
        w_hbm, *outs, weight, sems = refs[len(parts) :]
        copies = []
        for t in range(tiles):
            copy = pltpu.make_async_copy(
                w_hbm.at[:, pl.ds(start + t * tile, tile)], weight.at[t], sems.at[t]
            )
            copy.start()
            copies.append(copy)
        for t in range(tiles):
            copies[t].wait()
            at = 0
            for part in refs[: len(parts)]:
                size = part.shape[0]
                product = dot(part[...].reshape(size * rows, channels), weight[t])
                out, column = outs[t * tile // width], t * tile % width
                out[at : at + size, :, column : column + tile] = product.reshape(size, rows, tile)
                at += size

    vmem = pl.BlockSpec(memory_space=pltpu.VMEM)
    return pl.pallas_call(
        kernel,
        in_specs=[vmem] * len(parts) + [pl.BlockSpec(memory_space=pltpu.HBM)],
        out_specs=[vmem] * pieces,
        out_shape=[jax.ShapeDtypeStruct((chunks, rows, width), F32)] * pieces,
        scratch_shapes=[
            pltpu.VMEM((tiles, channels, tile), BF16),
            pltpu.SemaphoreType.DMA((tiles,)),
        ],
        compiler_params=params(40),
        cost_estimate=pl.CostEstimate(
            flops=2 * chunks * rows * channels * columns,
            bytes_accessed=2 * channels * columns + 4 * chunks * rows * columns,
            transcendentals=0,
        ),
        name="project",
    )(*parts, out_weight)


def line_tables(count):
    order, up, down = [], np.zeros((count, count), np.int32), np.zeros((count, count), np.int32)
    for me in range(count):
        def step(c):
            return count - c + me if c > me else (count + c - me if c < me else 10 * count)

        order.append(sorted(range(count), key=lambda c: (step(c), abs(c - me))))
        for s in range(1, count):
            if me < count - 1 and s > me:
                up[me, s] = order[me].index(count - s + me)
            if me > 0 and s > count - 1 - me:
                down[me, s] = order[me].index(s - count + me)
    return np.concatenate([np.array(order, np.int32), up, down], axis=1)


def sum_call(scal, mine, up, down, step):
    count, rows, width = mine.shape
    tile = min(1024, width)
    moving = pl.BlockSpec((1, rows, tile), lambda j, s: (0, 0, j))
    at_up, at_down = 2 + count + step, 2 + 2 * count + step

    def kernel(scal, a, b, c, d, out_up, out_down):
        out_up[...] = a[...] + c[...]
        out_down[...] = b[...] + d[...]

    return pl.pallas_call(
        kernel,
        grid_spec=pltpu.PrefetchScalarGridSpec(
            num_scalar_prefetch=1,
            grid=(width // tile,),
            in_specs=[
                pl.BlockSpec((1, rows, tile), lambda j, s: (s[at_up], 0, j)),
                pl.BlockSpec((1, rows, tile), lambda j, s: (s[at_down], 0, j)),
                moving,
                moving,
            ],
            out_specs=[moving, moving],
        ),
        out_shape=[jax.ShapeDtypeStruct(up.shape, F32)] * 2,
        cost_estimate=pl.CostEstimate(
            flops=10**10, bytes_accessed=24 * rows * width, transcendentals=0
        ),
        compiler_params=params(8),
        name="sum",
    )(scal, mine, mine, up, down)


def last_call(so_far, mine, up, down, first, wide):
    count, rows, width = mine.shape
    tile = min(512, width)
    moving = pl.BlockSpec((1, rows, tile), lambda j: (0, 0, j))

    def kernel(a, c, d, *refs):
        refs[-1][...] = (a[0] + c[0] + d[0]).astype(BF16)

    more = [] if so_far is None else [so_far]
    return pl.pallas_call(
        kernel,
        grid=(width // tile,),
        in_specs=[pl.BlockSpec((1, rows, tile), lambda j: (count - 1, 0, j)), moving, moving]
        + [pl.BlockSpec(memory_space=pl.ANY)] * len(more),
        out_specs=pl.BlockSpec((rows, tile), lambda j: (0, first // tile + j)),
        out_shape=jax.ShapeDtypeStruct((rows, wide), BF16),
        input_output_aliases={3: 0} if more else {},
        compiler_params=params(4),
        name="last_sum",
    )(mine, up, down, *more)


def send(to_up, to_down, step, axis):
    count = lax.axis_size(axis)
    return (
        lax.ppermute(to_up, axis, [(i, i + 1) for i in range(count - 1) if step > i]),
        lax.ppermute(to_down, axis, [(i, i - 1) for i in range(1, count) if step > count - 1 - i]),
    )


def body(
    features,
    gate_values,
    write_proj,
    read_proj,
    step_size,
    log_decay,
    starts,
    skip_weight,
    norm_gain,
    out_weight,
):
    tokens, channels = features.shape
    groups = write_proj.shape[1] // NSTATE
    count = lax.axis_size("ctx")
    chips = count // 2
    direct = channels % (128 * count) == 0 and chips & (chips - 1) == 0 and groups == 2
    me = lax.axis_index("ctx").astype(jnp.int32)
    place = jnp.stack([me % 2, me // 2]) if direct else jnp.zeros((2,), jnp.int32)
    line = lax.axis_size("head")
    table = jnp.asarray(line_tables(line))

    def scalars(table):
        return jnp.concatenate([place, table[lax.axis_index("head")]])

    rows = tokens // line

    inputs = (features, write_proj, step_size, log_decay, starts)
    chunks = chips if direct else 1
    other, pre_other = states_call(1, direct, *inputs, chunks, starts)
    mine, pre_mine = states_call(0, direct, *inputs, chunks, other)

    def intra(side, after):
        return intra_call(
            scal, side, features, write_proj, read_proj, step_size, log_decay, starts, skip_weight, after
        )

    if direct:
        theirs = over(other, "ctx")
        totals = chip_call(mine, theirs)
        totals, table = lax.optimization_barrier((totals, table))
        scal = scalars(table)
        moved = exchange(totals, "ctx")
        local = [intra(0, totals[0])]
        entries = prefix_call(moved, local[0][1])
        own = exchange(entries, "ctx")
        local += [intra(g, entries[0]) for g in range(1, groups)]
        fold = [fold_call([theirs], pre_mine, tokens)]
        own, mine, local, fold = lax.optimization_barrier((own, mine, local, fold))
        packed = pack_call(own, mine)
        entries = [packed, over(packed, "ctx")]
        fold.append(fold_call([entries[1]], pre_other, tokens, (1,)))
    else:
        scal = scalars(table)
        entries = [chain(mine, "ctx")[None], chain(other, "ctx")[None]]
        local = [intra(g, mine) for g in range(groups)]
        fold = [fold_call([], pre, tokens) for pre in (pre_mine, pre_other)]
    inner, reach = zip(*local)
    gain = norm_gain.reshape(1, channels)
    wide = out_weight.shape[1]
    pieces = 4
    size = wide // pieces
    early = 2
    firsts = []
    for sides in [[0], [1]] if groups > 1 else [[0, 1]]:
        at = sides[0]
        firsts = first_call(
            scal, sides, [entries[k] for k in sides], [fold[k] for k in sides], inner[at], reach[at], gate_values, read_proj,
            gain, out_weight, rows, size, early, firsts,
        )
    normed, *firsts = firsts
    moving = [send(f, f, 1, "head") for f in firsts]
    others = rest_call(scal, entries, fold, inner, reach, gate_values, read_proj, gain, rows)
    mine = [project_call([normed, others], out_weight, p * size, size)[0] for p in range(2)]
    late, mine, moving[0] = lax.optimization_barrier((normed, mine, moving[0]))
    firsts = project_call([late], out_weight, early * size, wide - early * size, pieces - early)
    moving += [send(f, f, 1, "head") for f in firsts]
    for p in range(2, pieces):
        later, moving[p] = lax.optimization_barrier((others, moving[p]))
        mine.append(project_call([normed, later], out_weight, p * size, size)[0])
    sums = None
    for s in range(2, line):
        for p in range(pieces):
            if sums is not None:
                mine[p], sums = lax.optimization_barrier((mine[p], sums))
            sums = sum_call(scal, mine[p], *moving[p], s)
            moving[p] = send(*sums, s, "head")
    result = None
    for p in range(pieces):
        result = last_call(result, mine[p], *moving[p], p * size, wide)
    return result


def solution(mesh):
    placed = (
        P("ctx", "head"),
        P("ctx", "head"),
        P("ctx", "head"),
        P("ctx", "head"),
        P("head", "ctx"),
        P("head", "ctx"),
        P("ctx"),
        P("head"),
        P("head"),
        P("head", None),
    )
    return jax.shard_map(
        body, mesh=mesh, in_specs=placed, out_specs=P(("ctx", "head"), None), check_vma=False
    )
```

```python
import jax
import jax.numpy as jnp
import numpy as np
from jax import lax
from jax.experimental import pallas as pl
from jax.experimental.pallas import tpu as pltpu
from jax.sharding import PartitionSpec as P

HEADS = 128
HEAD_DIM = 64
NSTATE = 128
GROUPS = 8
SPAN = 256
KROWS = 8
LOG2E = 1.4426950408889634
MIB = 1024 * 1024

eps = 1e-05
F32 = jnp.float32
BF16 = jnp.bfloat16


def three_parts(value, axis):
    high = value.astype(BF16)
    rest = value - high.astype(F32)
    middle = rest.astype(BF16)
    low = (rest - middle.astype(F32)).astype(BF16)
    return jnp.concatenate([high, middle, low], axis=axis)


def head_spread(heads, channels):
    row = lax.broadcasted_iota(jnp.int32, (3 * heads, channels), 0)
    col = lax.broadcasted_iota(jnp.int32, (3 * heads, channels), 1)
    return jnp.where(lax.rem(row, heads) == lax.div(col, HEAD_DIM), 1.0, 0.0).astype(BF16)


def dot(a, b, contract=((1,), (0,))):
    return lax.dot_general(a, b, (contract, ((), ())), preferred_element_type=F32)


def block_sums(decay, starts):
    heads = decay.shape[0]
    row = lax.broadcasted_iota(jnp.int32, (SPAN, SPAN), 0)
    col = lax.broadcasted_iota(jnp.int32, (SPAN, SPAN), 1)
    upper = jnp.where(row <= col, 1.0, 0.0).astype(BF16)
    begins = jnp.broadcast_to(starts.astype(F32), (16, SPAN)).astype(BF16)
    sums = dot(jnp.concatenate([three_parts(decay, 0), begins], axis=0), upper)
    cum = sums[:heads] + sums[heads : 2 * heads] + sums[2 * heads : 3 * heads]
    return cum, sums[3 * heads : 3 * heads + 8]


def position(direct):
    if not direct:
        return 0, 0
    me = lax.axis_index("ctx").astype(jnp.int32)
    return lax.rem(me, 2), lax.div(me, 2)


def cut(start, size, step=128):
    return pl.ds(start if isinstance(start, int) else pl.multiple_of(start, step), size)


def params(mib):
    return pltpu.CompilerParams(vmem_limit_bytes=mib * MIB)


def states_call(side, direct, features, write_proj, step_size, log_decay, starts, pieces, after):
    tokens, channels = features.shape
    groups = write_proj.shape[1] // NSTATE
    blocks = tokens // SPAN
    parts = max(1, groups // 2)
    heads, size = step_size.shape[0] // 2, channels // 2
    per_part, gch = heads // parts, size // parts
    width = size // pieces

    def kernel(
        feat_hbm, write_hbm, step_hbm, decay_hbm, starts_hbm, after, out, pre,
        feat, write, step, decay, starts, total, sems, write_sems, small_sems,
    ):
        core, _ = position(direct)
        half = core if side == 0 else 1 - core
        rows = cut(half * heads, heads, 8)
        small = [
            pltpu.make_async_copy(src, dst, small_sems.at[k])
            for k, (src, dst) in enumerate(
                [(decay_hbm.at[rows], decay), (starts_hbm, starts), (step_hbm.at[rows], step)]
            )
        ]
        for copy in small:
            copy.start()
        copies = []
        for part in range(parts):
            group = half * parts + part if groups > 1 else 0
            copy = pltpu.make_async_copy(
                write_hbm.at[:, cut(group * NSTATE, NSTATE)], write.at[part], write_sems.at[part]
            )
            copy.start()
            copies.append(copy)
            for block in range(blocks):
                copy = pltpu.make_async_copy(
                    feat_hbm.at[
                        pl.ds(block * SPAN, SPAN), cut(half * size + part * gch, gch)
                    ],
                    feat.at[part, block],
                    sems.at[part, block],
                )
                copy.start()
                copies.append(copy)
        spread = head_spread(per_part, gch)
        for copy in small:
            copy.wait()
        scales = []
        for block in range(blocks):
            span = slice(block * SPAN, (block + 1) * SPAN)
            cum, seg = block_sums(decay[:, span], starts[:, span])
            seg_last, last = seg[0:1, SPAN - 1 :], cum[:, SPAN - 1 :]
            tail = jnp.where(seg[0:1] == seg_last, jnp.exp(last - cum), 0.0) * step[:, span]
            keep = jnp.where(seg_last == 0.0, jnp.exp(last), 0.0)
            scales.append((tail, jnp.broadcast_to(keep, (heads, 128))))
        for part in range(parts):
            rows = slice(part * per_part, (part + 1) * per_part)
            lanes = slice(part * gch, (part + 1) * gch)
            copies.pop(0).wait()
            for block in range(blocks):
                tail, keep = scales[block]
                tail = dot(three_parts(tail[rows], 0), spread, ((0,), (0,)))
                keep = dot(three_parts(keep[rows], 0), spread, ((0,), (0,)))[:KROWS]
                copies.pop(0).wait()
                scaled = (tail * feat[part, block].astype(F32)).astype(BF16)
                state = dot(write[part, block * SPAN : (block + 1) * SPAN], scaled, ((0,), (0,)))
                if block > 0:
                    state = keep[0:1] * total[:NSTATE, lanes] + state
                    keep = keep * total[NSTATE:, lanes]
                total[:NSTATE, lanes] = state
                total[NSTATE:, lanes] = keep
                if block < blocks - 1:
                    pre[block, :NSTATE, lanes] = state
                    pre[block, NSTATE:, lanes] = keep
        for piece in range(pieces):
            out[piece] = total[:, piece * width : (piece + 1) * width]

    vmem = pl.BlockSpec(memory_space=pltpu.VMEM)
    return pl.pallas_call(
        kernel,
        in_specs=[pl.BlockSpec(memory_space=pltpu.HBM)] * 5 + [pl.BlockSpec(memory_space=pl.ANY)],
        out_specs=[vmem] * 2,
        scratch_shapes=[
            pltpu.VMEM((parts, blocks, SPAN, gch), BF16),
            pltpu.VMEM((parts, tokens, NSTATE), BF16),
            pltpu.VMEM((heads, tokens), F32),
            pltpu.VMEM((heads, tokens), F32),
            pltpu.VMEM((1, tokens), jnp.int32),
            pltpu.VMEM((NSTATE + KROWS, size), F32),
            pltpu.SemaphoreType.DMA((parts, blocks)),
            pltpu.SemaphoreType.DMA((parts,)),
            pltpu.SemaphoreType.DMA((3,)),
        ],
        out_shape=[
            jax.ShapeDtypeStruct((pieces, NSTATE + KROWS, width), F32),
            jax.ShapeDtypeStruct((blocks - 1, NSTATE + KROWS, size), F32),
        ],
        compiler_params=params(60 if side else 44),
        cost_estimate=pl.CostEstimate(flops=10**8, bytes_accessed=10**6, transcendentals=0),
        name="states",
    )(features, write_proj, step_size, log_decay, starts.reshape(1, tokens), after)


def intra_call(
    scal, side, features, write_proj, read_proj, step_size, log_decay, starts, skip_weight, out_weight,
    columns, after,
):
    tokens, channels = features.shape
    heads = step_size.shape[0]
    groups = write_proj.shape[1] // NSTATE
    per_group, gch = heads // groups, channels // groups
    blocks = tokens // SPAN
    half = SPAN // 2

    def group(s):
        return s[0] ^ side if groups > 1 else 0

    def kernel(
        scal, feat, write, read, step, decay, starts, skip, w_hbm, after, out, reach, weight, sem
    ):
        copy = pltpu.make_async_copy(
            w_hbm.at[cut(group(scal) * gch, gch), pl.ds(0, columns)], weight, sem
        )

        @pl.when(pl.program_id(0) == 0)
        def _():
            copy.start()

        cum, seg = block_sums(decay[...], starts[...])
        cum_log2 = cum * LOG2E
        vrow = cum_log2 - jnp.log2(step[...])
        far = jnp.where(seg[0:1] == 0.0, jnp.exp(cum), 0.0)
        fill = jnp.zeros((128 - 2 * per_group - 8, SPAN), F32)
        cols = jnp.concatenate([far, cum_log2, seg, fill], axis=0).T
        reach[...] = cols
        x = feat[...]
        scores = dot(read[...], write[...], ((1,), (1,)))
        row = lax.broadcasted_iota(jnp.int32, (SPAN, SPAN), 0)
        col = lax.broadcasted_iota(jnp.int32, (SPAN, SPAN), 1)
        together = (cols[:, 2 * per_group : 2 * per_group + 1] == seg[0:1]) & (row >= col)
        scores = jnp.where(together, scores, 0.0)
        own = skip[:, :per_group]
        for other in range(1, groups):
            theirs = skip[:, other * per_group : (other + 1) * per_group]
            own = jnp.where(group(scal) == other, theirs, own)
        own = jnp.broadcast_to(own, (8, per_group))
        skip_row = dot(three_parts(own, 1), head_spread(per_group, gch))[0:1]
        lane = lax.broadcasted_iota(jnp.int32, (SPAN, 2 * HEAD_DIM), 1)
        for pair in range(per_group // 2):
            part = slice(pair * 2 * HEAD_DIM, (pair + 1) * 2 * HEAD_DIM)
            xp = x[:, part]
            top = skip_row[:, part] * xp[:half].astype(F32)
            low = skip_row[:, part] * xp[half:].astype(F32)
            for which in range(2):
                head = 2 * pair + which
                mine = (lane >= HEAD_DIM) if which else (lane < HEAD_DIM)
                xh = jnp.where(mine, xp, jnp.zeros_like(xp))
                ci = cols[:, per_group + head : per_group + head + 1]
                vj = vrow[head : head + 1, :]
                w_top = jnp.exp2(jnp.minimum(ci[:half] - vj[:, :half], 1.0)) * scores[:half, :half]
                w_low = jnp.exp2(jnp.minimum(ci[half:] - vj, 1.0)) * scores[half:]
                top = top + dot(w_top.astype(BF16), xh[:half])
                low = low + dot(w_low.astype(BF16), xh)
            out[:half, part] = top
            out[half:, part] = low

        @pl.when(pl.program_id(0) == blocks - 1)
        def _():
            copy.wait()

    return pl.pallas_call(
        kernel,
        grid_spec=pltpu.PrefetchScalarGridSpec(
            num_scalar_prefetch=1,
            grid=(blocks,),
            in_specs=[
                pl.BlockSpec((SPAN, gch), lambda b, s: (b, group(s))),
                pl.BlockSpec((SPAN, NSTATE), lambda b, s: (b, group(s))),
                pl.BlockSpec((SPAN, NSTATE), lambda b, s: (b, group(s))),
                pl.BlockSpec((per_group, SPAN), lambda b, s: (group(s), b)),
                pl.BlockSpec((per_group, SPAN), lambda b, s: (group(s), b)),
                pl.BlockSpec((1, SPAN), lambda b, s: (0, b)),
                pl.BlockSpec((1, heads), lambda b, s: (0, 0)),
                pl.BlockSpec(memory_space=pltpu.HBM),
                pl.BlockSpec(memory_space=pl.ANY),
            ],
            out_specs=[
                pl.BlockSpec((SPAN, gch), lambda b, s: (b, 0)),
                pl.BlockSpec((SPAN, 128), lambda b, s: (b, 0)),
                pl.BlockSpec(memory_space=pl.ANY),
            ],
            scratch_shapes=[pltpu.SemaphoreType.DMA(())],
        ),
        out_shape=[
            jax.ShapeDtypeStruct((tokens, gch), F32),
            jax.ShapeDtypeStruct((tokens, 128), F32),
            jax.ShapeDtypeStruct((gch, columns), BF16),
        ],
        compiler_params=params(40),
        cost_estimate=pl.CostEstimate(flops=10**9, bytes_accessed=10**6, transcendentals=0),
        name="intra",
    )(
        scal,
        features,
        write_proj,
        read_proj,
        step_size,
        log_decay,
        starts.reshape(1, tokens),
        skip_weight.reshape(1, heads),
        out_weight,
        after,
    )


def chip_call(mine, theirs):
    pieces, rows, width = mine.shape

    def kernel(mine, theirs, *outs):
        core, chip = position(True)
        first_core = core == 0
        for offset in range(pieces):
            piece = chip ^ offset
            a, b = mine[piece], theirs[piece]
            first, second = jnp.where(first_core, a, b), jnp.where(first_core, b, a)
            keep = second[NSTATE:]
            outs[offset][:NSTATE] = keep[0:1] * first[:NSTATE] + second[:NSTATE]
            outs[offset][NSTATE:] = keep * first[NSTATE:]

    vmem = pl.BlockSpec(memory_space=pltpu.VMEM)
    return pl.pallas_call(
        kernel,
        in_specs=[vmem, vmem],
        out_specs=[vmem] * pieces,
        out_shape=[jax.ShapeDtypeStruct((rows, width), F32)] * pieces,
        compiler_params=params(6),
        name="chip_states",
    )(mine, theirs)


def prefix_call(parts, after):
    pieces, (rows, width) = len(parts), parts[0].shape

    def kernel(*refs):
        _, chip_here = position(True)
        ins, outs, stack = refs[:pieces], refs[pieces + 1 : 2 * pieces + 1], refs[2 * pieces + 1]
        for offset in range(pieces):
            stack[chip_here ^ offset] = ins[offset][...]
        entry = jnp.zeros((NSTATE, width), F32)
        for chip in range(pieces):
            state, keep = stack[chip, :NSTATE], stack[chip, NSTATE : NSTATE + 1]
            stack[chip, :NSTATE] = entry
            entry = keep * entry + state
        for offset in range(pieces):
            outs[offset][...] = stack[chip_here ^ offset, :NSTATE]

    vmem = pl.BlockSpec(memory_space=pltpu.VMEM)
    return pl.pallas_call(
        kernel,
        in_specs=[vmem] * pieces + [pl.BlockSpec(memory_space=pl.ANY)],
        out_specs=[vmem] * pieces,
        scratch_shapes=[pltpu.VMEM((pieces, rows, width), F32)],
        out_shape=[jax.ShapeDtypeStruct((NSTATE, width), F32)] * pieces,
        compiler_params=params(4),
        name="prefix",
    )(*parts, after)


def fold_call(theirs, pre, tokens, at=()):
    size = pre.shape[2]
    blocks = tokens // SPAN

    def kernel(*refs):
        pre, out = refs[-2:]
        state, keep = jnp.zeros((NSTATE, size), F32), jnp.ones((KROWS, size), F32)
        if theirs:
            core, _ = position(True)
            before = refs[0]
            before = jnp.concatenate(
                [before[(*at, p)] for p in range(theirs[0].shape[-3])], axis=1
            )
            state = jnp.where(core == 0, state, before[:NSTATE])
            keep = jnp.where(core == 0, keep, before[NSTATE:])
        out[0, :NSTATE] = state
        out[0, NSTATE:] = keep
        for block in range(1, blocks):
            here = pre[block - 1]
            out[block, :NSTATE] = here[NSTATE : NSTATE + 1] * state + here[:NSTATE]
            out[block, NSTATE:] = here[NSTATE:] * keep

    vmem = pl.BlockSpec(memory_space=pltpu.VMEM)
    return pl.pallas_call(
        kernel,
        in_specs=[vmem] * (len(theirs) + 1),
        out_specs=vmem,
        out_shape=jax.ShapeDtypeStruct((blocks, NSTATE + KROWS, size), F32),
        compiler_params=params(8),
        name="fold",
    )(*theirs, pre)


def pack_call(entries, mine):
    pieces, rows, width = mine.shape

    def kernel(*refs):
        mine, out = refs[-2:]
        for piece in range(pieces):
            out[0, piece, :NSTATE] = refs[piece][...]
            out[0, piece, NSTATE:] = jnp.zeros((rows - NSTATE, width), F32)
            out[1, piece] = mine[piece]

    vmem = pl.BlockSpec(memory_space=pltpu.VMEM)
    return pl.pallas_call(
        kernel,
        in_specs=[vmem] * (pieces + 1),
        out_specs=vmem,
        out_shape=jax.ShapeDtypeStruct((2, *mine.shape), F32),
        compiler_params=params(6),
        name="pack",
    )(*entries, mine)


def exchange(parts, axis):
    count = lax.axis_size(axis)
    return [parts[0]] + [
        lax.ppermute(parts[k], axis, [(i, i ^ (2 * k)) for i in range(count)])
        for k in range(1, len(parts))
    ]


def over(value, axis):
    return lax.ppermute(value, axis, [(i, i ^ 1) for i in range(lax.axis_size(axis))])


def chain(total, axis):
    count = lax.axis_size(axis)
    state, keep = total[:, :NSTATE], total[:, NSTATE : NSTATE + 1]
    steps = [(i, i + 1) for i in range(count - 1)]

    def step(index, incoming):
        return lax.ppermute(keep * incoming + state, axis, steps)

    return lax.fori_loop(0, count - 1, step, jnp.zeros_like(state))


def hold_entries(chip, entries, fold, held):
    pieces, _, width = held.shape
    for offset in range(pieces):
        piece = chip ^ offset
        part = cut(piece * width, width)
        entry = entries[0, offset, :NSTATE]
        held[piece] = (fold[NSTATE : NSTATE + 1, part] * entry + fold[:NSTATE, part]).astype(BF16)


def group_normed(held, c_rows, inner, reach, gate, gain):
    gch = inner.shape[1]
    per_group = gch // HEAD_DIM
    far = dot(three_parts(reach[:, :per_group], 1), head_spread(per_group, gch))
    carried = [dot(c_rows, piece) for piece in held]
    y = inner + far * (jnp.concatenate(carried, axis=1) if len(carried) > 1 else carried[0])
    g = gate.astype(F32)
    gated = y * (g / (1.0 + jnp.exp(-g)))
    mean_square = jnp.mean(gated * gated, axis=1, keepdims=True)
    return (gated * lax.rsqrt(mean_square + eps) * gain).astype(BF16)


def first_call(scal, sides, entries, fold, inner, reach, gate, read, gain, weight, rows, columns, before):
    tokens, channels = gate.shape
    gch = inner.shape[1]
    groups = channels // gch
    parts, width = entries[0].shape[1], entries[0].shape[3]
    wide = weight.shape[1]
    tile = min(512, columns)
    last = groups == 1 or bool(before)

    def group(s):
        return s[0] ^ sides[0] if groups > 1 else 0

    def kernel(scal, *refs):
        entry_refs, refs = refs[: len(sides)], refs[len(sides) :]
        folds, refs = refs[: len(sides)], refs[len(sides) :]
        inner, reach, read, gain, gate_hbm, weight = refs[:6]
        earlier, refs = refs[6 : 6 + len(before)], refs[6 + len(before) :]
        out, *firsts, gate, held, gate_sem = refs
        lanes = cut(group(scal) * gch, gch)
        gate_copy = pltpu.make_async_copy(
            gate_hbm.at[cut(scal[2] * rows, rows, rows), lanes], gate, gate_sem
        )
        gate_copy.start()
        for k in range(len(sides)):
            hold_entries(scal[1], entry_refs[k], folds[k].at[0], held.at[k])
        gate_copy.wait()
        pieces = [held[k, p] for k in range(len(sides)) for p in range(parts)]
        normed = group_normed(pieces, read[...], inner[...], reach[...], gate[...], gain[...])
        if last:
            out[0, :, lanes] = normed
            if before:
                out[0, :, cut((1 - group(scal)) * gch, gch)] = earlier[0][...]
        else:
            out[...] = normed
        for t in range(wide // tile):
            here = slice(t * tile, (t + 1) * tile)
            product = dot(normed, weight[:, here])
            if not last:
                firsts[0][:, here] = product
                continue
            if before:
                product = product + earlier[1][:, here]
            at = t * tile % columns
            firsts[t * tile // columns][0, :, at : at + tile] = product

    def whole(value):
        zeros = (0,) * value.ndim
        return pl.BlockSpec(value.shape, lambda j, s: zeros)

    def chunk(size):
        return pl.BlockSpec((rows, size), lambda j, s: (s[2], 0))

    if last:
        shapes = [((1, rows, channels), BF16)] + [((1, rows, columns), F32)] * (wide // columns)
    else:
        shapes = [((rows, gch), BF16), ((rows, wide), F32)]
    return pl.pallas_call(
        kernel,
        grid_spec=pltpu.PrefetchScalarGridSpec(
            num_scalar_prefetch=1,
            grid=(1,),
            in_specs=[whole(v) for v in entries]
            + [pl.BlockSpec((1, *f.shape[1:]), lambda j, s: (lax.div(s[2] * rows, SPAN), 0, 0)) for f in fold]
            + [
                chunk(gch),
                chunk(128),
                pl.BlockSpec((rows, NSTATE), lambda j, s: (s[2], group(s))),
                pl.BlockSpec((1, gch), lambda j, s: (0, group(s))),
                pl.BlockSpec(memory_space=pltpu.HBM),
                pl.BlockSpec(memory_space=pltpu.VMEM),
            ]
            + [whole(v) for v in before],
            out_specs=[
                pl.BlockSpec(shape, lambda j, s, zeros=(0,) * len(shape): zeros) for shape, _ in shapes
            ],
            scratch_shapes=[
                pltpu.VMEM((rows, gch), BF16),
                pltpu.VMEM((len(sides), parts, NSTATE, width), BF16),
                pltpu.SemaphoreType.DMA(()),
            ],
        ),
        out_shape=[jax.ShapeDtypeStruct(shape, kind) for shape, kind in shapes],
        compiler_params=params(16),
        name="first",
    )(scal, *entries, *fold, inner, reach, read, gain, gate, weight, *before)


def rest_call(scal, entries, fold, inner, reach, gate, read, gain, rows):
    tokens, channels = gate.shape
    groups, parts, width = len(inner), entries[0].shape[1], entries[0].shape[3]
    count, blocks = tokens // rows, tokens // SPAN
    gch = channels // groups

    def kernel(scal, *refs):
        entry_refs, refs = refs[:2], refs[2:]
        inner, reach, refs = refs[:groups], refs[groups : 2 * groups], refs[2 * groups :]
        folds, refs = refs[:2], refs[2:]
        gate_hbm, read, gain, out, gate, held, sems = refs
        step = pl.program_id(0)

        def gate_copy(k):
            first_row = pl.multiple_of(scal[3 + k] * rows, rows)
            return pltpu.make_async_copy(gate_hbm.at[pl.ds(first_row, rows)], gate.at[k], sems.at[k])

        @pl.when(step == 0)
        def _():
            for k in range(count - 1):
                gate_copy(k).start()
            for block in range(blocks):
                for side in range(2):
                    hold_entries(scal[1], entry_refs[side], folds[side].at[block], held.at[block, side])

        gate_copy(step).wait()
        blk = lax.div(scal[3 + step] * rows, SPAN)
        for k in range(groups):
            group = scal[0] ^ k if groups > 1 else 0
            sides = [k] if groups > 1 else [0, 1]
            pieces = [held[blk, side, p] for side in sides for p in range(parts)]
            lanes = cut(group * gch, gch)
            c_rows = read[:, cut(group * NSTATE, NSTATE)]
            out[0, :, lanes] = group_normed(
                pieces, c_rows, inner[k][...], reach[k][...], gate[step, :, lanes], gain[:, lanes]
            )

    def whole(value):
        zeros = (0,) * value.ndim
        return pl.BlockSpec(value.shape, lambda j, s: zeros)

    def chunk(size):
        return pl.BlockSpec((rows, size), lambda j, s: (s[3 + j], 0))

    return pl.pallas_call(
        kernel,
        grid_spec=pltpu.PrefetchScalarGridSpec(
            num_scalar_prefetch=1,
            grid=(count - 1,),
            in_specs=[whole(v) for v in entries]
            + [chunk(gch)] * groups
            + [chunk(128)] * groups
            + [whole(f) for f in fold]
            + [pl.BlockSpec(memory_space=pltpu.HBM)]
            + [chunk(groups * NSTATE), whole(gain)],
            out_specs=pl.BlockSpec((1, rows, channels), lambda j, s: (j, 0, 0)),
            scratch_shapes=[
                pltpu.VMEM((count - 1, rows, channels), BF16),
                pltpu.VMEM((blocks, 2, parts, NSTATE, width), BF16),
                pltpu.SemaphoreType.DMA((count - 1,)),
            ],
        ),
        out_shape=jax.ShapeDtypeStruct((count - 1, rows, channels), BF16),
        compiler_params=params(14),
        cost_estimate=pl.CostEstimate(flops=10**9, bytes_accessed=10**6, transcendentals=0),
        name="rest",
    )(scal, *entries, *inner, *reach, *fold, gate, read, gain)


def project_call(parts, out_weight, start, columns, pieces=1):
    chunks, rows, channels = sum(p.shape[0] for p in parts), *parts[0].shape[1:]
    width = columns // pieces
    tile = min(512, width)
    tiles = columns // tile

    def kernel(*refs):
        w_hbm, *outs, weight, sems = refs[len(parts) :]
        copies = []
        for t in range(tiles):
            copy = pltpu.make_async_copy(
                w_hbm.at[:, pl.ds(start + t * tile, tile)], weight.at[t], sems.at[t]
            )
            copy.start()
            copies.append(copy)
        for t in range(tiles):
            copies[t].wait()
            at = 0
            for part in refs[: len(parts)]:
                size = part.shape[0]
                product = dot(part[...].reshape(size * rows, channels), weight[t])
                out, column = outs[t * tile // width], t * tile % width
                out[at : at + size, :, column : column + tile] = product.reshape(size, rows, tile)
                at += size

    vmem = pl.BlockSpec(memory_space=pltpu.VMEM)
    return pl.pallas_call(
        kernel,
        in_specs=[vmem] * len(parts) + [pl.BlockSpec(memory_space=pltpu.HBM)],
        out_specs=[vmem] * pieces,
        out_shape=[jax.ShapeDtypeStruct((chunks, rows, width), F32)] * pieces,
        scratch_shapes=[
            pltpu.VMEM((tiles, channels, tile), BF16),
            pltpu.SemaphoreType.DMA((tiles,)),
        ],
        compiler_params=params(40),
        cost_estimate=pl.CostEstimate(
            flops=2 * chunks * rows * channels * columns,
            bytes_accessed=2 * channels * columns + 4 * chunks * rows * columns,
            transcendentals=0,
        ),
        name="project",
    )(*parts, out_weight)


def line_tables(count):
    order, up, down = [], np.zeros((count, count), np.int32), np.zeros((count, count), np.int32)
    for me in range(count):
        def step(c):
            return count - c + me if c > me else (count + c - me if c < me else 10 * count)

        order.append(sorted(range(count), key=lambda c: (step(c), abs(c - me))))
        for s in range(1, count):
            if me < count - 1 and s > me:
                up[me, s] = order[me].index(count - s + me)
            if me > 0 and s > count - 1 - me:
                down[me, s] = order[me].index(s - count + me)
    return np.concatenate([np.array(order, np.int32), up, down], axis=1)


def sum_call(scal, mine, up, down, step):
    count, rows, width = mine.shape
    tile = min(1024, width)
    moving = pl.BlockSpec((1, rows, tile), lambda j, s: (0, 0, j))
    at_up, at_down = 2 + count + step, 2 + 2 * count + step

    def kernel(scal, a, b, c, d, out_up, out_down):
        out_up[...] = a[...] + c[...]
        out_down[...] = b[...] + d[...]

    return pl.pallas_call(
        kernel,
        grid_spec=pltpu.PrefetchScalarGridSpec(
            num_scalar_prefetch=1,
            grid=(width // tile,),
            in_specs=[
                pl.BlockSpec((1, rows, tile), lambda j, s: (s[at_up], 0, j)),
                pl.BlockSpec((1, rows, tile), lambda j, s: (s[at_down], 0, j)),
                moving,
                moving,
            ],
            out_specs=[moving, moving],
        ),
        out_shape=[jax.ShapeDtypeStruct(up.shape, F32)] * 2,
        cost_estimate=pl.CostEstimate(
            flops=10**10, bytes_accessed=24 * rows * width, transcendentals=0
        ),
        compiler_params=params(8),
        name="sum",
    )(scal, mine, mine, up, down)


def last_call(so_far, mine, up, down, first, wide):
    count, rows, width = mine.shape
    tile = min(512, width)
    moving = pl.BlockSpec((1, rows, tile), lambda j: (0, 0, j))

    def kernel(a, c, d, *refs):
        refs[-1][...] = (a[0] + c[0] + d[0]).astype(BF16)

    more = [] if so_far is None else [so_far]
    return pl.pallas_call(
        kernel,
        grid=(width // tile,),
        in_specs=[pl.BlockSpec((1, rows, tile), lambda j: (count - 1, 0, j)), moving, moving]
        + [pl.BlockSpec(memory_space=pl.ANY)] * len(more),
        out_specs=pl.BlockSpec((rows, tile), lambda j: (0, first // tile + j)),
        out_shape=jax.ShapeDtypeStruct((rows, wide), BF16),
        input_output_aliases={3: 0} if more else {},
        compiler_params=params(4),
        name="last_sum",
    )(mine, up, down, *more)


def send(to_up, to_down, step, axis):
    count = lax.axis_size(axis)
    return (
        lax.ppermute(to_up, axis, [(i, i + 1) for i in range(count - 1) if step > i]),
        lax.ppermute(to_down, axis, [(i, i - 1) for i in range(1, count) if step > count - 1 - i]),
    )


def body(
    features,
    gate_values,
    write_proj,
    read_proj,
    step_size,
    log_decay,
    starts,
    skip_weight,
    norm_gain,
    out_weight,
):
    tokens, channels = features.shape
    groups = write_proj.shape[1] // NSTATE
    count = lax.axis_size("ctx")
    chips = count // 2
    direct = channels % (128 * count) == 0 and chips & (chips - 1) == 0 and groups == 2
    me = lax.axis_index("ctx").astype(jnp.int32)
    place = jnp.stack([me % 2, me // 2]) if direct else jnp.zeros((2,), jnp.int32)
    line = lax.axis_size("head")
    table = jnp.asarray(line_tables(line))

    def scalars(table):
        return jnp.concatenate([place, table[lax.axis_index("head")]])

    rows = tokens // line

    inputs = (features, write_proj, step_size, log_decay, starts)
    chunks = chips if direct else 1
    other, pre_other = states_call(1, direct, *inputs, chunks, starts)
    mine, pre_mine = states_call(0, direct, *inputs, chunks, other)

    wide = out_weight.shape[1]
    pieces = 4
    size = wide // pieces
    early = 2

    def intra(side, after):
        return intra_call(
            scal, side, features, write_proj, read_proj, step_size, log_decay, starts, skip_weight,
            out_weight, early * size, after,
        )

    if direct:
        theirs = over(other, "ctx")
        totals = chip_call(mine, theirs)
        totals, table = lax.optimization_barrier((totals, table))
        scal = scalars(table)
        moved = exchange(totals, "ctx")
        local = [intra(0, totals[0])]
        entries = prefix_call(moved, local[0][1])
        own = exchange(entries, "ctx")
        local += [intra(g, entries[0]) for g in range(1, groups)]
        fold = [fold_call([theirs], pre_mine, tokens)]
        own, mine, local, fold = lax.optimization_barrier((own, mine, local, fold))
        packed = pack_call(own, mine)
        entries = [packed, over(packed, "ctx")]
        fold.append(fold_call([entries[1]], pre_other, tokens, (1,)))
    else:
        scal = scalars(table)
        entries = [chain(mine, "ctx")[None], chain(other, "ctx")[None]]
        local = [intra(g, mine) for g in range(groups)]
        fold = [fold_call([], pre, tokens) for pre in (pre_mine, pre_other)]
    inner, reach, weights = zip(*local)
    gain = norm_gain.reshape(1, channels)
    firsts = []
    for sides in [[0], [1]] if groups > 1 else [[0, 1]]:
        at = sides[0]
        firsts = first_call(
            scal, sides, [entries[k] for k in sides], [fold[k] for k in sides], inner[at], reach[at], gate_values, read_proj,
            gain, weights[at], rows, size, firsts,
        )
    normed, *firsts = firsts
    moving = [send(f, f, 1, "head") for f in firsts]
    others = rest_call(scal, entries, fold, inner, reach, gate_values, read_proj, gain, rows)
    mine = [project_call([normed, others], out_weight, p * size, size)[0] for p in range(2)]
    late, mine, moving[0] = lax.optimization_barrier((normed, mine, moving[0]))
    firsts = project_call([late], out_weight, early * size, wide - early * size, pieces - early)
    moving += [send(f, f, 1, "head") for f in firsts]
    for p in range(2, pieces):
        later, moving[p] = lax.optimization_barrier((others, moving[p]))
        mine.append(project_call([normed, later], out_weight, p * size, size)[0])
    sums = None
    for s in range(2, line):
        for p in range(pieces):
            turn = (s - 1) * pieces + p
            if sums is not None:
                mine[p], sums = lax.optimization_barrier((mine[p], sums))
            if turn >= 6:
                back = (turn - 2) % pieces
                mine[p], moving[back] = lax.optimization_barrier((mine[p], moving[back]))
            sums = sum_call(scal, mine[p], *moving[p], s)
            moving[p] = send(*sums, s, "head")
    result = None
    for p in range(pieces):
        result = last_call(result, mine[p], *moving[p], p * size, wide)
    return result


def solution(mesh):
    placed = (
        P("ctx", "head"),
        P("ctx", "head"),
        P("ctx", "head"),
        P("ctx", "head"),
        P("head", "ctx"),
        P("head", "ctx"),
        P("ctx"),
        P("head"),
        P("head"),
        P("head", None),
    )
    return jax.shard_map(
        body, mesh=mesh, in_specs=placed, out_specs=P(("ctx", "head"), None), check_vma=False
    )
```

```python
import jax
import jax.numpy as jnp
import numpy as np
from jax import lax
from jax.experimental import pallas as pl
from jax.experimental.pallas import tpu as pltpu
from jax.sharding import PartitionSpec as P

HEADS = 128
HEAD_DIM = 64
NSTATE = 128
GROUPS = 8
SPAN = 256
KROWS = 8
LOG2E = 1.4426950408889634
MIB = 1024 * 1024

eps = 1e-05
F32 = jnp.float32
BF16 = jnp.bfloat16


def three_parts(value, axis):
    high = value.astype(BF16)
    rest = value - high.astype(F32)
    middle = rest.astype(BF16)
    low = (rest - middle.astype(F32)).astype(BF16)
    return jnp.concatenate([high, middle, low], axis=axis)


def head_spread(heads, channels):
    row = lax.broadcasted_iota(jnp.int32, (3 * heads, channels), 0)
    col = lax.broadcasted_iota(jnp.int32, (3 * heads, channels), 1)
    return jnp.where(lax.rem(row, heads) == lax.div(col, HEAD_DIM), 1.0, 0.0).astype(BF16)


def dot(a, b, contract=((1,), (0,))):
    return lax.dot_general(a, b, (contract, ((), ())), preferred_element_type=F32)


def block_sums(decay, starts):
    heads = decay.shape[0]
    row = lax.broadcasted_iota(jnp.int32, (SPAN, SPAN), 0)
    col = lax.broadcasted_iota(jnp.int32, (SPAN, SPAN), 1)
    upper = jnp.where(row <= col, 1.0, 0.0).astype(BF16)
    begins = jnp.broadcast_to(starts.astype(F32), (16, SPAN)).astype(BF16)
    sums = dot(jnp.concatenate([three_parts(decay, 0), begins], axis=0), upper)
    cum = sums[:heads] + sums[heads : 2 * heads] + sums[2 * heads : 3 * heads]
    return cum, sums[3 * heads : 3 * heads + 8]


def position(direct):
    if not direct:
        return 0, 0
    me = lax.axis_index("ctx").astype(jnp.int32)
    return lax.rem(me, 2), lax.div(me, 2)


def cut(start, size, step=128):
    return pl.ds(start if isinstance(start, int) else pl.multiple_of(start, step), size)


def params(mib):
    return pltpu.CompilerParams(vmem_limit_bytes=mib * MIB)


def states_call(side, direct, features, write_proj, step_size, log_decay, starts, pieces, after):
    tokens, channels = features.shape
    groups = write_proj.shape[1] // NSTATE
    blocks = tokens // SPAN
    parts = max(1, groups // 2)
    heads, size = step_size.shape[0] // 2, channels // 2
    per_part, gch = heads // parts, size // parts
    width = size // pieces

    def kernel(
        feat_hbm, write_hbm, step_hbm, decay_hbm, starts_hbm, after, out, pre,
        feat, write, step, decay, starts, total, sems, write_sems, small_sems,
    ):
        core, _ = position(direct)
        half = core if side == 0 else 1 - core
        rows = cut(half * heads, heads, 8)
        small = [
            pltpu.make_async_copy(src, dst, small_sems.at[k])
            for k, (src, dst) in enumerate(
                [(decay_hbm.at[rows], decay), (starts_hbm, starts), (step_hbm.at[rows], step)]
            )
        ]
        for copy in small:
            copy.start()
        copies = []
        for part in range(parts):
            group = half * parts + part if groups > 1 else 0
            copy = pltpu.make_async_copy(
                write_hbm.at[:, cut(group * NSTATE, NSTATE)], write.at[part], write_sems.at[part]
            )
            copy.start()
            copies.append(copy)
            for block in range(blocks):
                copy = pltpu.make_async_copy(
                    feat_hbm.at[
                        pl.ds(block * SPAN, SPAN), cut(half * size + part * gch, gch)
                    ],
                    feat.at[part, block],
                    sems.at[part, block],
                )
                copy.start()
                copies.append(copy)
        spread = head_spread(per_part, gch)
        for copy in small[:2]:
            copy.wait()
        scales = []
        for block in range(blocks):
            span = slice(block * SPAN, (block + 1) * SPAN)
            cum, seg = block_sums(decay[:, span], starts[:, span])
            seg_last, last = seg[0:1, SPAN - 1 :], cum[:, SPAN - 1 :]
            if block == 0:
                small[2].wait()
            tail = jnp.where(seg[0:1] == seg_last, jnp.exp(last - cum), 0.0) * step[:, span]
            keep = jnp.where(seg_last == 0.0, jnp.exp(last), 0.0)
            scales.append((tail, jnp.broadcast_to(keep, (heads, 128))))
        for part in range(parts):
            rows = slice(part * per_part, (part + 1) * per_part)
            lanes = slice(part * gch, (part + 1) * gch)
            copies.pop(0).wait()
            for block in range(blocks):
                tail, keep = scales[block]
                tail = dot(three_parts(tail[rows], 0), spread, ((0,), (0,)))
                keep = dot(three_parts(keep[rows], 0), spread, ((0,), (0,)))[:KROWS]
                copies.pop(0).wait()
                scaled = (tail * feat[part, block].astype(F32)).astype(BF16)
                state = dot(write[part, block * SPAN : (block + 1) * SPAN], scaled, ((0,), (0,)))
                if block > 0:
                    state = keep[0:1] * total[:NSTATE, lanes] + state
                    keep = keep * total[NSTATE:, lanes]
                total[:NSTATE, lanes] = state
                total[NSTATE:, lanes] = keep
                if block < blocks - 1:
                    pre[block, :NSTATE, lanes] = state
                    pre[block, NSTATE:, lanes] = keep
        for piece in range(pieces):
            out[piece] = total[:, piece * width : (piece + 1) * width]

    vmem = pl.BlockSpec(memory_space=pltpu.VMEM)
    return pl.pallas_call(
        kernel,
        in_specs=[pl.BlockSpec(memory_space=pltpu.HBM)] * 5 + [pl.BlockSpec(memory_space=pl.ANY)],
        out_specs=[vmem] * 2,
        scratch_shapes=[
            pltpu.VMEM((parts, blocks, SPAN, gch), BF16),
            pltpu.VMEM((parts, tokens, NSTATE), BF16),
            pltpu.VMEM((heads, tokens), F32),
            pltpu.VMEM((heads, tokens), F32),
            pltpu.VMEM((1, tokens), jnp.int32),
            pltpu.VMEM((NSTATE + KROWS, size), F32),
            pltpu.SemaphoreType.DMA((parts, blocks)),
            pltpu.SemaphoreType.DMA((parts,)),
            pltpu.SemaphoreType.DMA((3,)),
        ],
        out_shape=[
            jax.ShapeDtypeStruct((pieces, NSTATE + KROWS, width), F32),
            jax.ShapeDtypeStruct((blocks - 1, NSTATE + KROWS, size), F32),
        ],
        compiler_params=params(60 if side else 44),
        cost_estimate=pl.CostEstimate(flops=10**8, bytes_accessed=10**6, transcendentals=0),
        name="states",
    )(features, write_proj, step_size, log_decay, starts.reshape(1, tokens), after)


def intra_call(
    scal, side, features, write_proj, read_proj, step_size, log_decay, starts, skip_weight, out_weight,
    columns, after,
):
    tokens, channels = features.shape
    heads = step_size.shape[0]
    groups = write_proj.shape[1] // NSTATE
    per_group, gch = heads // groups, channels // groups
    blocks = tokens // SPAN
    half = SPAN // 2

    def group(s):
        return s[0] ^ side if groups > 1 else 0

    def kernel(
        scal, feat, write, read, step, decay, starts, skip, w_hbm, after, out, reach, weight, sem
    ):
        copy = pltpu.make_async_copy(
            w_hbm.at[cut(group(scal) * gch, gch), pl.ds(0, columns)], weight, sem
        )

        @pl.when(pl.program_id(0) == 0)
        def _():
            copy.start()

        cum, seg = block_sums(decay[...], starts[...])
        cum_log2 = cum * LOG2E
        vrow = cum_log2 - jnp.log2(step[...])
        far = jnp.where(seg[0:1] == 0.0, jnp.exp(cum), 0.0)
        fill = jnp.zeros((128 - 2 * per_group - 8, SPAN), F32)
        cols = jnp.concatenate([far, cum_log2, seg, fill], axis=0).T
        reach[...] = cols
        x = feat[...]
        scores = dot(read[...], write[...], ((1,), (1,)))
        row = lax.broadcasted_iota(jnp.int32, (SPAN, SPAN), 0)
        col = lax.broadcasted_iota(jnp.int32, (SPAN, SPAN), 1)
        together = (cols[:, 2 * per_group : 2 * per_group + 1] == seg[0:1]) & (row >= col)
        scores = jnp.where(together, scores, 0.0)
        own = skip[:, :per_group]
        for other in range(1, groups):
            theirs = skip[:, other * per_group : (other + 1) * per_group]
            own = jnp.where(group(scal) == other, theirs, own)
        own = jnp.broadcast_to(own, (8, per_group))
        skip_row = dot(three_parts(own, 1), head_spread(per_group, gch))[0:1]
        lane = lax.broadcasted_iota(jnp.int32, (SPAN, 2 * HEAD_DIM), 1)
        for pair in range(per_group // 2):
            part = slice(pair * 2 * HEAD_DIM, (pair + 1) * 2 * HEAD_DIM)
            xp = x[:, part]
            top = skip_row[:, part] * xp[:half].astype(F32)
            low = skip_row[:, part] * xp[half:].astype(F32)
            for which in range(2):
                head = 2 * pair + which
                mine = (lane >= HEAD_DIM) if which else (lane < HEAD_DIM)
                xh = jnp.where(mine, xp, jnp.zeros_like(xp))
                ci = cols[:, per_group + head : per_group + head + 1]
                vj = vrow[head : head + 1, :]
                w_top = jnp.exp2(jnp.minimum(ci[:half] - vj[:, :half], 1.0)) * scores[:half, :half]
                w_low = jnp.exp2(jnp.minimum(ci[half:] - vj, 1.0)) * scores[half:]
                top = top + dot(w_top.astype(BF16), xh[:half])
                low = low + dot(w_low.astype(BF16), xh)
            out[:half, part] = top
            out[half:, part] = low

        @pl.when(pl.program_id(0) == blocks - 1)
        def _():
            copy.wait()

    return pl.pallas_call(
        kernel,
        grid_spec=pltpu.PrefetchScalarGridSpec(
            num_scalar_prefetch=1,
            grid=(blocks,),
            in_specs=[
                pl.BlockSpec((SPAN, gch), lambda b, s: (b, group(s))),
                pl.BlockSpec((SPAN, NSTATE), lambda b, s: (b, group(s))),
                pl.BlockSpec((SPAN, NSTATE), lambda b, s: (b, group(s))),
                pl.BlockSpec((per_group, SPAN), lambda b, s: (group(s), b)),
                pl.BlockSpec((per_group, SPAN), lambda b, s: (group(s), b)),
                pl.BlockSpec((1, SPAN), lambda b, s: (0, b)),
                pl.BlockSpec((1, heads), lambda b, s: (0, 0)),
                pl.BlockSpec(memory_space=pltpu.HBM),
                pl.BlockSpec(memory_space=pl.ANY),
            ],
            out_specs=[
                pl.BlockSpec((SPAN, gch), lambda b, s: (b, 0)),
                pl.BlockSpec((SPAN, 128), lambda b, s: (b, 0)),
                pl.BlockSpec(memory_space=pl.ANY),
            ],
            scratch_shapes=[pltpu.SemaphoreType.DMA(())],
        ),
        out_shape=[
            jax.ShapeDtypeStruct((tokens, gch), F32),
            jax.ShapeDtypeStruct((tokens, 128), F32),
            jax.ShapeDtypeStruct((gch, columns), BF16),
        ],
        compiler_params=params(40),
        cost_estimate=pl.CostEstimate(flops=10**9, bytes_accessed=10**6, transcendentals=0),
        name="intra",
    )(
        scal,
        features,
        write_proj,
        read_proj,
        step_size,
        log_decay,
        starts.reshape(1, tokens),
        skip_weight.reshape(1, heads),
        out_weight,
        after,
    )


def chip_call(mine, theirs):
    pieces, rows, width = mine.shape

    def kernel(mine, theirs, *outs):
        core, chip = position(True)
        first_core = core == 0
        for offset in range(pieces):
            piece = chip ^ offset
            a, b = mine[piece], theirs[piece]
            first, second = jnp.where(first_core, a, b), jnp.where(first_core, b, a)
            keep = second[NSTATE:]
            outs[offset][:NSTATE] = keep[0:1] * first[:NSTATE] + second[:NSTATE]
            outs[offset][NSTATE:] = keep * first[NSTATE:]

    vmem = pl.BlockSpec(memory_space=pltpu.VMEM)
    return pl.pallas_call(
        kernel,
        in_specs=[vmem, vmem],
        out_specs=[vmem] * pieces,
        out_shape=[jax.ShapeDtypeStruct((rows, width), F32)] * pieces,
        compiler_params=params(6),
        name="chip_states",
    )(mine, theirs)


def prefix_call(parts, after):
    pieces, (rows, width) = len(parts), parts[0].shape

    def kernel(*refs):
        _, chip_here = position(True)
        ins, outs, stack = refs[:pieces], refs[pieces + 1 : 2 * pieces + 1], refs[2 * pieces + 1]
        for offset in range(pieces):
            stack[chip_here ^ offset] = ins[offset][...]
        entry = jnp.zeros((NSTATE, width), F32)
        for chip in range(pieces):
            state, keep = stack[chip, :NSTATE], stack[chip, NSTATE : NSTATE + 1]
            stack[chip, :NSTATE] = entry
            entry = keep * entry + state
        for offset in range(pieces):
            outs[offset][...] = stack[chip_here ^ offset, :NSTATE]

    vmem = pl.BlockSpec(memory_space=pltpu.VMEM)
    return pl.pallas_call(
        kernel,
        in_specs=[vmem] * pieces + [pl.BlockSpec(memory_space=pl.ANY)],
        out_specs=[vmem] * pieces,
        scratch_shapes=[pltpu.VMEM((pieces, rows, width), F32)],
        out_shape=[jax.ShapeDtypeStruct((NSTATE, width), F32)] * pieces,
        compiler_params=params(4),
        name="prefix",
    )(*parts, after)


def fold_call(theirs, pre, tokens, at=()):
    size = pre.shape[2]
    blocks = tokens // SPAN

    def kernel(*refs):
        pre, out = refs[-2:]
        state, keep = jnp.zeros((NSTATE, size), F32), jnp.ones((KROWS, size), F32)
        if theirs:
            core, _ = position(True)
            before = refs[0]
            before = jnp.concatenate(
                [before[(*at, p)] for p in range(theirs[0].shape[-3])], axis=1
            )
            state = jnp.where(core == 0, state, before[:NSTATE])
            keep = jnp.where(core == 0, keep, before[NSTATE:])
        out[0, :NSTATE] = state
        out[0, NSTATE:] = keep
        for block in range(1, blocks):
            here = pre[block - 1]
            out[block, :NSTATE] = here[NSTATE : NSTATE + 1] * state + here[:NSTATE]
            out[block, NSTATE:] = here[NSTATE:] * keep

    vmem = pl.BlockSpec(memory_space=pltpu.VMEM)
    return pl.pallas_call(
        kernel,
        in_specs=[vmem] * (len(theirs) + 1),
        out_specs=vmem,
        out_shape=jax.ShapeDtypeStruct((blocks, NSTATE + KROWS, size), F32),
        compiler_params=params(8),
        name="fold",
    )(*theirs, pre)


def pack_call(entries, mine):
    pieces, rows, width = mine.shape

    def kernel(*refs):
        mine, out = refs[-2:]
        for piece in range(pieces):
            out[0, piece, :NSTATE] = refs[piece][...]
            out[0, piece, NSTATE:] = jnp.zeros((rows - NSTATE, width), F32)
            out[1, piece] = mine[piece]

    vmem = pl.BlockSpec(memory_space=pltpu.VMEM)
    return pl.pallas_call(
        kernel,
        in_specs=[vmem] * (pieces + 1),
        out_specs=vmem,
        out_shape=jax.ShapeDtypeStruct((2, *mine.shape), F32),
        compiler_params=params(6),
        name="pack",
    )(*entries, mine)


def exchange(parts, axis):
    count = lax.axis_size(axis)
    return [parts[0]] + [
        lax.ppermute(parts[k], axis, [(i, i ^ (2 * k)) for i in range(count)])
        for k in range(1, len(parts))
    ]


def over(value, axis):
    return lax.ppermute(value, axis, [(i, i ^ 1) for i in range(lax.axis_size(axis))])


def chain(total, axis):
    count = lax.axis_size(axis)
    state, keep = total[:, :NSTATE], total[:, NSTATE : NSTATE + 1]
    steps = [(i, i + 1) for i in range(count - 1)]

    def step(index, incoming):
        return lax.ppermute(keep * incoming + state, axis, steps)

    return lax.fori_loop(0, count - 1, step, jnp.zeros_like(state))


def hold_entries(chip, entries, fold, held):
    pieces, _, width = held.shape
    for offset in range(pieces):
        piece = chip ^ offset
        part = cut(piece * width, width)
        entry = entries[0, offset, :NSTATE]
        held[piece] = (fold[NSTATE : NSTATE + 1, part] * entry + fold[:NSTATE, part]).astype(BF16)


def group_normed(held, c_rows, inner, reach, gate, gain):
    gch = inner.shape[1]
    per_group = gch // HEAD_DIM
    far = dot(three_parts(reach[:, :per_group], 1), head_spread(per_group, gch))
    carried = [dot(c_rows, piece) for piece in held]
    y = inner + far * (jnp.concatenate(carried, axis=1) if len(carried) > 1 else carried[0])
    g = gate.astype(F32)
    gated = y * (g / (1.0 + jnp.exp(-g)))
    mean_square = jnp.mean(gated * gated, axis=1, keepdims=True)
    return (gated * lax.rsqrt(mean_square + eps) * gain).astype(BF16)


def first_call(scal, sides, entries, fold, inner, reach, gate, read, gain, weight, rows, columns, before):
    tokens, channels = gate.shape
    gch = inner.shape[1]
    groups = channels // gch
    parts, width = entries[0].shape[1], entries[0].shape[3]
    wide = weight.shape[1]
    tile = min(512, columns)
    last = groups == 1 or bool(before)

    def group(s):
        return s[0] ^ sides[0] if groups > 1 else 0

    def kernel(scal, *refs):
        entry_refs, refs = refs[: len(sides)], refs[len(sides) :]
        folds, refs = refs[: len(sides)], refs[len(sides) :]
        inner, reach, read, gain, gate_hbm, weight = refs[:6]
        earlier, refs = refs[6 : 6 + len(before)], refs[6 + len(before) :]
        out, *firsts, gate, held, gate_sem = refs
        lanes = cut(group(scal) * gch, gch)
        gate_copy = pltpu.make_async_copy(
            gate_hbm.at[cut(scal[2] * rows, rows, rows), lanes], gate, gate_sem
        )
        gate_copy.start()
        for k in range(len(sides)):
            hold_entries(scal[1], entry_refs[k], folds[k].at[0], held.at[k])
        gate_copy.wait()
        pieces = [held[k, p] for k in range(len(sides)) for p in range(parts)]
        normed = group_normed(pieces, read[...], inner[...], reach[...], gate[...], gain[...])
        if last:
            out[0, :, lanes] = normed
            if before:
                out[0, :, cut((1 - group(scal)) * gch, gch)] = earlier[0][...]
        else:
            out[...] = normed
        for t in range(wide // tile):
            here = slice(t * tile, (t + 1) * tile)
            product = dot(normed, weight[:, here])
            if not last:
                firsts[0][:, here] = product
                continue
            if before:
                product = product + earlier[1][:, here]
            at = t * tile % columns
            firsts[t * tile // columns][0, :, at : at + tile] = product

    def whole(value):
        zeros = (0,) * value.ndim
        return pl.BlockSpec(value.shape, lambda j, s: zeros)

    def chunk(size):
        return pl.BlockSpec((rows, size), lambda j, s: (s[2], 0))

    if last:
        shapes = [((1, rows, channels), BF16)] + [((1, rows, columns), F32)] * (wide // columns)
    else:
        shapes = [((rows, gch), BF16), ((rows, wide), F32)]
    return pl.pallas_call(
        kernel,
        grid_spec=pltpu.PrefetchScalarGridSpec(
            num_scalar_prefetch=1,
            grid=(1,),
            in_specs=[whole(v) for v in entries]
            + [pl.BlockSpec((1, *f.shape[1:]), lambda j, s: (lax.div(s[2] * rows, SPAN), 0, 0)) for f in fold]
            + [
                chunk(gch),
                chunk(128),
                pl.BlockSpec((rows, NSTATE), lambda j, s: (s[2], group(s))),
                pl.BlockSpec((1, gch), lambda j, s: (0, group(s))),
                pl.BlockSpec(memory_space=pltpu.HBM),
                pl.BlockSpec(memory_space=pltpu.VMEM),
            ]
            + [whole(v) for v in before],
            out_specs=[
                pl.BlockSpec(shape, lambda j, s, zeros=(0,) * len(shape): zeros) for shape, _ in shapes
            ],
            scratch_shapes=[
                pltpu.VMEM((rows, gch), BF16),
                pltpu.VMEM((len(sides), parts, NSTATE, width), BF16),
                pltpu.SemaphoreType.DMA(()),
            ],
        ),
        out_shape=[jax.ShapeDtypeStruct(shape, kind) for shape, kind in shapes],
        compiler_params=params(16),
        name="first",
    )(scal, *entries, *fold, inner, reach, read, gain, gate, weight, *before)


def rest_call(scal, entries, fold, inner, reach, gate, read, gain, rows):
    tokens, channels = gate.shape
    groups, parts, width = len(inner), entries[0].shape[1], entries[0].shape[3]
    count, blocks = tokens // rows, tokens // SPAN
    gch = channels // groups

    def kernel(scal, *refs):
        entry_refs, refs = refs[:2], refs[2:]
        inner, reach, refs = refs[:groups], refs[groups : 2 * groups], refs[2 * groups :]
        folds, refs = refs[:2], refs[2:]
        gate_hbm, read, gain, out, gate, held, sems = refs
        step = pl.program_id(0)

        def gate_copy(k):
            first_row = pl.multiple_of(scal[3 + k] * rows, rows)
            return pltpu.make_async_copy(gate_hbm.at[pl.ds(first_row, rows)], gate.at[k], sems.at[k])

        @pl.when(step == 0)
        def _():
            for k in range(count - 1):
                gate_copy(k).start()
            for block in range(blocks):
                for side in range(2):
                    hold_entries(scal[1], entry_refs[side], folds[side].at[block], held.at[block, side])

        gate_copy(step).wait()
        blk = lax.div(scal[3 + step] * rows, SPAN)
        for k in range(groups):
            group = scal[0] ^ k if groups > 1 else 0
            sides = [k] if groups > 1 else [0, 1]
            pieces = [held[blk, side, p] for side in sides for p in range(parts)]
            lanes = cut(group * gch, gch)
            c_rows = read[:, cut(group * NSTATE, NSTATE)]
            out[0, :, lanes] = group_normed(
                pieces, c_rows, inner[k][...], reach[k][...], gate[step, :, lanes], gain[:, lanes]
            )

    def whole(value):
        zeros = (0,) * value.ndim
        return pl.BlockSpec(value.shape, lambda j, s: zeros)

    def chunk(size):
        return pl.BlockSpec((rows, size), lambda j, s: (s[3 + j], 0))

    return pl.pallas_call(
        kernel,
        grid_spec=pltpu.PrefetchScalarGridSpec(
            num_scalar_prefetch=1,
            grid=(count - 1,),
            in_specs=[whole(v) for v in entries]
            + [chunk(gch)] * groups
            + [chunk(128)] * groups
            + [whole(f) for f in fold]
            + [pl.BlockSpec(memory_space=pltpu.HBM)]
            + [chunk(groups * NSTATE), whole(gain)],
            out_specs=pl.BlockSpec((1, rows, channels), lambda j, s: (j, 0, 0)),
            scratch_shapes=[
                pltpu.VMEM((count - 1, rows, channels), BF16),
                pltpu.VMEM((blocks, 2, parts, NSTATE, width), BF16),
                pltpu.SemaphoreType.DMA((count - 1,)),
            ],
        ),
        out_shape=jax.ShapeDtypeStruct((count - 1, rows, channels), BF16),
        compiler_params=params(14),
        cost_estimate=pl.CostEstimate(flops=10**9, bytes_accessed=10**6, transcendentals=0),
        name="rest",
    )(scal, *entries, *inner, *reach, *fold, gate, read, gain)


def project_call(parts, out_weight, start, columns, pieces=1):
    chunks, rows, channels = sum(p.shape[0] for p in parts), *parts[0].shape[1:]
    width = columns // pieces
    tile = min(512, width)
    tiles = columns // tile

    def kernel(*refs):
        w_hbm, *outs, weight, sems = refs[len(parts) :]
        copies = []
        for t in range(tiles):
            copy = pltpu.make_async_copy(
                w_hbm.at[:, pl.ds(start + t * tile, tile)], weight.at[t], sems.at[t]
            )
            copy.start()
            copies.append(copy)
        for t in range(tiles):
            copies[t].wait()
            at = 0
            for part in refs[: len(parts)]:
                size = part.shape[0]
                product = dot(part[...].reshape(size * rows, channels), weight[t])
                out, column = outs[t * tile // width], t * tile % width
                out[at : at + size, :, column : column + tile] = product.reshape(size, rows, tile)
                at += size

    vmem = pl.BlockSpec(memory_space=pltpu.VMEM)
    return pl.pallas_call(
        kernel,
        in_specs=[vmem] * len(parts) + [pl.BlockSpec(memory_space=pltpu.HBM)],
        out_specs=[vmem] * pieces,
        out_shape=[jax.ShapeDtypeStruct((chunks, rows, width), F32)] * pieces,
        scratch_shapes=[
            pltpu.VMEM((tiles, channels, tile), BF16),
            pltpu.SemaphoreType.DMA((tiles,)),
        ],
        compiler_params=params(40),
        cost_estimate=pl.CostEstimate(
            flops=2 * chunks * rows * channels * columns,
            bytes_accessed=2 * channels * columns + 4 * chunks * rows * columns,
            transcendentals=0,
        ),
        name="project",
    )(*parts, out_weight)


def line_tables(count):
    order, up, down = [], np.zeros((count, count), np.int32), np.zeros((count, count), np.int32)
    for me in range(count):
        def step(c):
            return count - c + me if c > me else (count + c - me if c < me else 10 * count)

        order.append(sorted(range(count), key=lambda c: (step(c), abs(c - me))))
        for s in range(1, count):
            if me < count - 1 and s > me:
                up[me, s] = order[me].index(count - s + me)
            if me > 0 and s > count - 1 - me:
                down[me, s] = order[me].index(s - count + me)
    return np.concatenate([np.array(order, np.int32), up, down], axis=1)


def sum_call(scal, mine, up, down, step):
    count, rows, width = mine.shape
    tile = min(1024, width)
    moving = pl.BlockSpec((1, rows, tile), lambda j, s: (0, 0, j))
    at_up, at_down = 2 + count + step, 2 + 2 * count + step

    def kernel(scal, a, b, c, d, out_up, out_down):
        out_up[...] = a[...] + c[...]
        out_down[...] = b[...] + d[...]

    return pl.pallas_call(
        kernel,
        grid_spec=pltpu.PrefetchScalarGridSpec(
            num_scalar_prefetch=1,
            grid=(width // tile,),
            in_specs=[
                pl.BlockSpec((1, rows, tile), lambda j, s: (s[at_up], 0, j)),
                pl.BlockSpec((1, rows, tile), lambda j, s: (s[at_down], 0, j)),
                moving,
                moving,
            ],
            out_specs=[moving, moving],
        ),
        out_shape=[jax.ShapeDtypeStruct(up.shape, F32)] * 2,
        cost_estimate=pl.CostEstimate(
            flops=10**10, bytes_accessed=24 * rows * width, transcendentals=0
        ),
        compiler_params=params(8),
        name="sum",
    )(scal, mine, mine, up, down)


def last_call(so_far, mine, up, down, first, wide):
    count, rows, width = mine.shape
    tile = min(1024, width)
    moving = pl.BlockSpec((1, rows, tile), lambda j: (0, 0, j))

    def kernel(a, c, d, *refs):
        refs[-1][...] = (a[0] + c[0] + d[0]).astype(BF16)

    more = [] if so_far is None else [so_far]
    return pl.pallas_call(
        kernel,
        grid=(width // tile,),
        in_specs=[pl.BlockSpec((1, rows, tile), lambda j: (count - 1, 0, j)), moving, moving]
        + [pl.BlockSpec(memory_space=pl.ANY)] * len(more),
        out_specs=pl.BlockSpec((rows, tile), lambda j: (0, first // tile + j)),
        out_shape=jax.ShapeDtypeStruct((rows, wide), BF16),
        input_output_aliases={3: 0} if more else {},
        compiler_params=params(4),
        name="last_sum",
    )(mine, up, down, *more)


def send(to_up, to_down, step, axis):
    count = lax.axis_size(axis)
    return (
        lax.ppermute(to_up, axis, [(i, i + 1) for i in range(count - 1) if step > i]),
        lax.ppermute(to_down, axis, [(i, i - 1) for i in range(1, count) if step > count - 1 - i]),
    )


def body(
    features,
    gate_values,
    write_proj,
    read_proj,
    step_size,
    log_decay,
    starts,
    skip_weight,
    norm_gain,
    out_weight,
):
    tokens, channels = features.shape
    groups = write_proj.shape[1] // NSTATE
    count = lax.axis_size("ctx")
    chips = count // 2
    direct = channels % (128 * count) == 0 and chips & (chips - 1) == 0 and groups == 2
    me = lax.axis_index("ctx").astype(jnp.int32)
    place = jnp.stack([me % 2, me // 2]) if direct else jnp.zeros((2,), jnp.int32)
    line = lax.axis_size("head")
    table = jnp.asarray(line_tables(line))

    def scalars(table):
        return jnp.concatenate([place, table[lax.axis_index("head")]])

    rows = tokens // line

    inputs = (features, write_proj, step_size, log_decay, starts)
    chunks = chips if direct else 1
    other, pre_other = states_call(1, direct, *inputs, chunks, starts)
    mine, pre_mine = states_call(0, direct, *inputs, chunks, other)

    wide = out_weight.shape[1]
    pieces = 4
    size = wide // pieces
    early = 2

    def intra(side, after):
        return intra_call(
            scal, side, features, write_proj, read_proj, step_size, log_decay, starts, skip_weight,
            out_weight, early * size, after,
        )

    if direct:
        theirs = over(other, "ctx")
        totals = chip_call(mine, theirs)
        totals, table = lax.optimization_barrier((totals, table))
        scal = scalars(table)
        moved = exchange(totals, "ctx")
        local = [intra(0, totals[0])]
        entries = prefix_call(moved, local[0][1])
        own = exchange(entries, "ctx")
        local += [intra(g, entries[0]) for g in range(1, groups)]
        fold = [fold_call([theirs], pre_mine, tokens)]
        own, mine, local, fold = lax.optimization_barrier((own, mine, local, fold))
        packed = pack_call(own, mine)
        entries = [packed, over(packed, "ctx")]
        fold.append(fold_call([entries[1]], pre_other, tokens, (1,)))
    else:
        scal = scalars(table)
        entries = [chain(mine, "ctx")[None], chain(other, "ctx")[None]]
        local = [intra(g, mine) for g in range(groups)]
        fold = [fold_call([], pre, tokens) for pre in (pre_mine, pre_other)]
    inner, reach, weights = zip(*local)
    gain = norm_gain.reshape(1, channels)
    firsts = []
    for sides in [[0], [1]] if groups > 1 else [[0, 1]]:
        at = sides[0]
        firsts = first_call(
            scal, sides, [entries[k] for k in sides], [fold[k] for k in sides], inner[at], reach[at], gate_values, read_proj,
            gain, weights[at], rows, size, firsts,
        )
    normed, *firsts = firsts
    moving = [send(f, f, 1, "head") for f in firsts]
    others = rest_call(scal, entries, fold, inner, reach, gate_values, read_proj, gain, rows)
    mine = [project_call([normed, others], out_weight, p * size, size)[0] for p in range(2)]
    late, mine, moving[0] = lax.optimization_barrier((normed, mine, moving[0]))
    firsts = project_call([late], out_weight, early * size, wide - early * size, pieces - early)
    moving += [send(f, f, 1, "head") for f in firsts]
    for p in range(2, pieces):
        later, moving[p] = lax.optimization_barrier((others, moving[p]))
        mine.append(project_call([normed, later], out_weight, p * size, size)[0])
    sums = None
    for s in range(2, line):
        for p in range(pieces):
            turn = (s - 1) * pieces + p
            if sums is not None:
                mine[p], sums = lax.optimization_barrier((mine[p], sums))
            if turn >= 6:
                back = (turn - 2) % pieces
                mine[p], moving[back] = lax.optimization_barrier((mine[p], moving[back]))
            sums = sum_call(scal, mine[p], *moving[p], s)
            moving[p] = send(*sums, s, "head")
    result = None
    for p in range(pieces):
        result = last_call(result, mine[p], *moving[p], p * size, wide)
    return result


def solution(mesh):
    placed = (
        P("ctx", "head"),
        P("ctx", "head"),
        P("ctx", "head"),
        P("ctx", "head"),
        P("head", "ctx"),
        P("head", "ctx"),
        P("ctx"),
        P("head"),
        P("head"),
        P("head", None),
    )
    return jax.shard_map(
        body, mesh=mesh, in_specs=placed, out_specs=P(("ctx", "head"), None), check_vma=False
    )
```
